256 devices in a mesh: dev: 256 (over z, y, x, core).
Axes of the slice: x: 4, y: 4, z: 8, core: 2. Of those that a mesh axis runs over, the one named last changes fastest.
Arguments:
- points: float32 [8, 524288], P(None, 'dev'), as said below
- noise: float32 [524288], P('dev'), may hold values from 0.3 to 3
- pattern: int32 [256, 6], P('dev'), may hold values from 0 to 1, as said below
- solution: float32 [16, 524288], P(None, 'dev'), may hold values from -6 to 6
- residual: float32 [16, 524288], P(None, 'dev'), may hold values from -12 to 12
- direction: float32 [16, 524288], P(None, 'dev'), may hold values from -12 to 12
Outputs:
- new_solution: float32 [16, 524288], P(None, 'dev')
- new_residual: float32 [16, 524288], P(None, 'dev')
- new_direction: float32 [16, 524288], P(None, 'dev')
The draws below stay inside these ranges and needn't reach their ends.
Inputs may be any that keep to these rules, and one draw needn't show every extreme that they name: pattern[i, o - 1] is 1 exactly where some point of block i and some point of block i + o may lie within distance 1 in the first coordinate, 0 where i + o >= 256; some row has a 1 in its last column. points of block i have a first coordinate in an interval that lies after block i - 1's; where pattern[i, o - 1] is 0, and for blocks more than 6 apart, the first coordinates of the two blocks differ by 1 or more; the other coordinates lie in [0, 1).
All inputs are finite; a program needn't handle non-finite values.
Results may differ from the reference program's by a relative error of at most 0.0003.
Values sent between devices are 32-bit elements; how exact they have to be, the bound alone decides.
A program may use at most 64 MiB of HBM per device.

```python
import math
import jax
import jax.numpy as jnp
from jax import lax

DIMS = 8
RHS = 16
BLOCK = 2048
REACH = 6
POINTS = 524288
N_DEV = 256


def block_layout(key):
    index = jnp.arange(N_DEV)
    widths = jax.random.randint(jax.random.fold_in(key, 1), (N_DEV,), 1, 4)
    run_sizes = jax.random.randint(jax.random.fold_in(key, 2), (N_DEV,), 1, REACH + 2)
    forced = jax.random.randint(jax.random.fold_in(key, 3), (), 0, 4)
    run_sizes = jnp.where(index == forced, REACH + 1, run_sizes)
    bounds = jnp.cumsum(run_sizes) - run_sizes
    starts = jnp.any(index[:, None] == bounds[None, :], axis=1)
    jumps = jax.random.randint(jax.random.fold_in(key, 4), (N_DEV,), 60, 121)
    jumps = jnp.where(starts, jumps, 0)
    offsets = jnp.cumsum(widths + jumps) - widths
    return (widths, offsets)


def rising_ramp():
    place = jnp.arange(POINTS).astype(jnp.float32) / (POINTS - 1)
    return jnp.exp(math.log(3.0) * place)[None, :]


def smooth_part():
    place = jnp.arange(POINTS).astype(jnp.float32) / (POINTS - 1)
    row = jnp.arange(RHS).astype(jnp.float32)[:, None] / RHS
    return 0.6 + 0.3 * jnp.cos(2.0 * math.pi * (5.0 * place[None, :] + row))


def draw_pattern(key, part):
    widths, offsets = block_layout(key)
    index = jnp.arange(N_DEV)
    columns = []
    for offset in range(1, REACH + 1):
        other = jnp.minimum(index + offset, N_DEV - 1)
        gap = offsets[other] - (offsets + widths)
        columns.append(((index + offset < N_DEV) & (gap < 60)).astype(jnp.int32))
    return jnp.stack(columns, axis=1)


def draw_points(key, part):
    widths, offsets = block_layout(key)
    key = jax.random.fold_in(key, 12)
    first = jax.random.uniform(jax.random.fold_in(key, 1), (POINTS,), jnp.float32)
    rest = jax.random.uniform(jax.random.fold_in(key, 2), (DIMS - 1, POINTS), jnp.float32)
    owner = jnp.arange(POINTS) // BLOCK
    lead = (offsets[owner].astype(jnp.float32) + widths[owner].astype(jnp.float32) * first) / 60.0
    rest = jnp.minimum(rest, 0.9999)
    return jnp.concatenate([lead[None, :], rest], axis=0)


def draw_residual(key, part):
    key = jax.random.fold_in(key, 13)
    base = jnp.clip(jax.random.normal(key, (RHS, POINTS), jnp.float32), -4.0, 4.0)
    return base * rising_ramp()


def draw_direction(key, part):
    key = jax.random.fold_in(key, 14)
    base = jnp.clip(jax.random.normal(key, (RHS, POINTS), jnp.float32), -3.0, 3.0)
    return (base + smooth_part()) * rising_ramp()


def steps_of(own_key, extent, pieces, least, largest):
    gain = 1.0
    for axis_at, parts in pieces:
        steps = jax.random.uniform(jax.random.fold_in(jax.random.fold_in(own_key, 6), axis_at), (parts,), jnp.float32, least / len(pieces), largest / len(pieces))
        gain = gain * jnp.repeat(jnp.exp(steps), extent[axis_at] // parts).reshape((-1,) + (1,) * (len(extent) - 1 - axis_at))
    return gain


def centred(key, extent, scale, bound, cuts=(), kind=jnp.bfloat16):
    factor_of = steps_of(key, extent, cuts, -0.22, 0.18) if cuts else 1.0
    array = jax.random.normal(key, extent, jnp.float32) * scale * factor_of
    return jnp.minimum(jnp.maximum(array, -bound), bound).astype(kind)


def setup_inputs(seed: int = 0) -> dict:
    arg_keys = jax.random.split(jax.random.key(seed), 7)
    points = draw_points(jax.random.fold_in(arg_keys[6], 71), 0)
    noise = jnp.clip(jnp.exp(math.log(3.0) - 2.3025851 * jax.random.uniform(arg_keys[1], (POINTS,), jnp.float32) ** steps_of(arg_keys[1], (POINTS,), ((0, 256),), -0.2, 0.2)), 0.3, 3.0)
    pattern = draw_pattern(jax.random.fold_in(arg_keys[6], 71), 0)
    solution = centred(arg_keys[3], (RHS, POINTS), 1.0, 6.0, ((1, 256),), jnp.float32)
    residual = draw_residual(jax.random.fold_in(arg_keys[6], 71), 0)
    direction = draw_direction(jax.random.fold_in(arg_keys[6], 71), 0)
    return dict(points=points, noise=noise, pattern=pattern, solution=solution, residual=residual, direction=direction)


def kern_tile(left_points, right_points):
    dist_sq = jnp.zeros((left_points.shape[1], right_points.shape[1]), jnp.float32)
    for coord in range(left_points.shape[0]):
        diff = left_points[coord][:, None] - right_points[coord][None, :]
        dist_sq = dist_sq + diff * diff
    dist = jnp.sqrt(dist_sq)
    tail = jnp.maximum(1.0 - dist, 0.0)
    return tail ** 7 * (7.0 * dist + 1.0)

def reference(points, noise, pattern, solution, residual, direction):
    blocks = N_DEV
    pts = points.reshape(DIMS, blocks, BLOCK).transpose(1, 0, 2)
    dirs = direction.reshape(RHS, blocks, BLOCK).transpose(1, 0, 2)
    index = jnp.arange(blocks, dtype=jnp.int32)
    hp = lax.Precision.HIGHEST

    def diag_term(i):
        tile = kern_tile(pts[i], pts[i])
        return lax.dot_general(dirs[i], tile, (((1,), (1,)), ((), ())), precision=hp, preferred_element_type=jnp.float32)
    image_blocks = lax.map(diag_term, index)
    for offset in range(1, REACH + 1):

        def pair_term(i):
            other = jnp.minimum(i + offset, blocks - 1).astype(jnp.int32)
            tile = kern_tile(pts[i], pts[other])
            near = lax.dot_general(dirs[other], tile, (((1,), (1,)), ((), ())), precision=hp, preferred_element_type=jnp.float32)
            far = jnp.dot(dirs[i], tile, precision=hp, preferred_element_type=jnp.float32)
            return (near, far)
        near, far = lax.map(pair_term, index)
        flag = (pattern[:, offset - 1] > 0).astype(jnp.float32)[:, None, None]
        image_blocks = image_blocks + flag * near
        moved = jnp.concatenate([jnp.zeros((offset, RHS, BLOCK), jnp.float32), (flag * far)[:blocks - offset]], axis=0)
        image_blocks = image_blocks + moved
    image = image_blocks.transpose(1, 0, 2).reshape(RHS, blocks * BLOCK) + noise[None, :] * direction
    norm_now = lax.optimization_barrier(jnp.sum(residual * residual, axis=1))
    curv = lax.optimization_barrier(jnp.sum(direction * image, axis=1))
    alpha = norm_now / curv
    new_solution = solution + alpha[:, None] * direction
    new_residual = residual - alpha[:, None] * image
    fresh = lax.optimization_barrier(jnp.sum(new_residual * new_residual, axis=1))
    beta = fresh / (norm_now + 1e-05)
    new_direction = new_residual + beta[:, None] * direction
    return (new_solution, new_residual, new_direction)
```

```python
import functools

import jax
import jax.numpy as jnp
from jax import lax
from jax.experimental import pallas as pl
from jax.experimental.pallas import tpu as pltpu
from jax.sharding import PartitionSpec as P

F = jnp.float32
BF = jnp.bfloat16
MESH = pl.DeviceIdType.MESH
DIMS = 8
RHS = 16
N = 2048
SLOTS = 6
DEVS = 256
DEPTH = 64
C = 256
GROUP = 16
OFFSETS = (1, 2, 3, -4, -5, -6)
VMEM_LIMIT = 48 * 2**20


def split2(x):
    high = x.astype(BF)
    low = (x - high.astype(F)).astype(BF)
    return high.astype(F), low.astype(F)


def split3(x):
    high = x.astype(BF).astype(F)
    rest = x - high
    mid = rest.astype(BF).astype(F)
    low = (rest - mid).astype(BF).astype(F)
    return high, mid, low


def features(points, centre, skip_first):
    row = lax.broadcasted_iota(jnp.int32, points.shape, 0)
    x = jnp.where(row == 0, 0.0 if skip_first else points - centre, points - 0.5)
    norm = jnp.sum(x * x, axis=0, keepdims=True)
    a, b, c = split3(x)
    na, nb, nc = split3(norm)
    ones = jnp.where(row < 3, 1.0, 0.0)
    ones2 = jnp.where((row >= 3) & (row < 6), 1.0, 0.0)
    here = jnp.where(
        row == 0, na, jnp.where(row == 1, nb, jnp.where(row == 2, nc, ones2))
    )
    there = jnp.where(
        row == 3, na, jnp.where(row == 4, nb, jnp.where(row == 5, nc, ones))
    )
    zero = jnp.zeros_like(x)
    left = jnp.concatenate([a, a, b, b, a, c, here, zero], axis=0)
    right = jnp.concatenate(
        [-2.0 * a, -2.0 * b, -2.0 * a, -2.0 * b, -2.0 * c, -2.0 * a, there, zero],
        axis=0,
    )
    return left, right


def kern(dist_sq):
    u = jnp.maximum(dist_sq, 1e-30)
    s = u * lax.rsqrt(u)
    t = jnp.maximum(1.0 - s, 0.0)
    t2 = t * t
    t4 = t2 * t2
    t7 = t4 * (t2 * t)
    return t7 * (8.0 / 7.0 - t)


def halves(v):
    high = v.astype(BF)
    low = (v - high.astype(F)).astype(BF)
    return high, low


def dot(a, b):
    return jnp.dot(a, b, preferred_element_type=F)


def gather_kernel(
    points, noise, direction, got_points, got_dir, image,
    left, right, rows, cols, near, column, send_sem, recv_sem,
):
    me = lax.axis_index("dev")
    barrier = pltpu.get_barrier_semaphore()
    for offset in OFFSETS:
        for signed in (offset, -offset):
            pl.semaphore_signal(
                barrier,
                inc=1,
                device_id=(lax.rem(me + signed + DEVS, DEVS),),
                device_id_type=MESH,
            )
    pl.semaphore_wait(barrier, 2 * SLOTS)
    copies = []
    for slot, offset in enumerate(OFFSETS):
        to = lax.rem(me - offset + DEVS, DEVS)
        for part, (src, dst) in enumerate(
            ((points, got_points.at[slot]), (direction, got_dir.at[slot]))
        ):
            copy = pltpu.make_async_remote_copy(
                src_ref=src,
                dst_ref=dst,
                send_sem=send_sem.at[slot, part],
                recv_sem=recv_sem.at[slot, part],
                device_id=(to,),
                device_id_type=MESH,
            )
            copy.start()
            copies.append(copy)

    a, b = features(points[...], 0.0, True)
    left[...] = a.T.astype(BF)
    right[...] = b.astype(BF)
    both = jnp.concatenate(split2(direction[...] * 7.0), axis=0)
    rows[...] = both.astype(BF)
    cols[...] = both.T.astype(BF)
    first = points[0:1, :]
    column[...] = jnp.broadcast_to(first, (8, N)).T
    near[...] = jnp.zeros_like(near)
    image[...] = noise[...] * direction[...]

    def square(at_row, at_col):
        d = dot(left[at_row, :], right[:, at_col])
        x = column[at_row, 0:1] - points[0:1, at_col]
        high, low = halves(kern(d + x * x))
        w = cols[at_col, :]
        near[at_row, :] += dot(high, w) + dot(low, w)
        return high, low

    def one_column(j, carry):
        at_col = pl.ds(pl.multiple_of(j * C, C), C)

        def one_row(i, acc):
            at_row = pl.ds(pl.multiple_of(i * C, C), C)
            high, low = square(at_row, at_col)
            mine = rows[:, at_row]
            return acc + dot(mine, high) + dot(mine, low)

        far = lax.fori_loop(0, j, one_row, jnp.zeros((2 * RHS, C), F))
        square(at_col, at_col)
        image[:, at_col] += far[:RHS] + far[RHS:]
        return carry

    lax.fori_loop(0, N // C, one_column, 0)
    turned = near[...].T
    image[...] += turned[:RHS] + turned[RHS:]
    for copy in copies:
        copy.wait()


def pair_kernel(
    pattern, points, direction, got_points, got_dir, start, image, far_out,
    left, right, rows, cols, near, column,
):
    first = points[0:1, :]
    least, most = jnp.min(first), jnp.max(first)
    centre = 0.5 * least + 0.5 * most
    both = jnp.concatenate(split2(direction[...] * 7.0), axis=0)
    rows[...] = both.astype(BF)
    near[...] = jnp.zeros_like(near)

    def products(at_row, at_col, dist_sq):
        high, low = halves(kern(dist_sq))
        w = cols[at_col, :]
        near[at_row, :] += dot(high, w) + dot(low, w)
        mine = rows[:, at_row]
        far = dot(mine, high) + dot(mine, low)
        return far[:RHS] + far[RHS:]

    def set_left(skip_first):
        a, _ = features(points[...], centre, skip_first)
        left[...] = a.T.astype(BF)

    set_left(False)
    spread_own = most - least

    def one_slot(slot, carry):
        theirs = got_points[slot, 0:1, :]
        low, high = jnp.min(theirs), jnp.max(theirs)
        own_flag = pattern[0, jnp.minimum(slot, 2)] > 0
        touch = (
            (low - most < 1.0) & (least - high < 1.0) & ((slot > 2) | own_flag)
        )
        reach = jnp.maximum(jnp.maximum(high - centre, centre - low), spread_own)
        narrow = reach <= 1.5

        @pl.when(jnp.logical_not(touch))
        def _():
            far_out[slot] = jnp.zeros((RHS, N), F)

        @pl.when(touch)
        def _():
            vis = jnp.concatenate(split2(got_dir[slot] * 7.0), axis=0)
            cols[...] = vis.T.astype(BF)

        @pl.when(touch & narrow)
        def _():
            _, b = features(got_points[slot], centre, False)
            right[...] = b.astype(BF)

            def one_column(j, c):
                at_col = pl.ds(pl.multiple_of(j * C, C), C)
                d = dot(left[...], right[:, at_col])
                far_out[slot, :, at_col] = products(pl.ds(0, N), at_col, d)
                return c

            lax.fori_loop(0, N // C, one_column, 0)

        @pl.when(touch & jnp.logical_not(narrow))
        def _():
            set_left(True)
            column[...] = jnp.broadcast_to(first, (8, N)).T
            _, b = features(got_points[slot], centre, True)
            right[...] = b.astype(BF)

            def one_column(j, c):
                at_col = pl.ds(pl.multiple_of(j * C, C), C)

                def one_row(i, acc):
                    at_row = pl.ds(pl.multiple_of(i * C, C), C)
                    d = dot(left[at_row, :], right[:, at_col])
                    x = column[at_row, 0:1] - got_points[slot, 0:1, at_col]
                    return acc + products(at_row, at_col, d + x * x)

                far_out[slot, :, at_col] = lax.fori_loop(
                    0, N // C, one_row, jnp.zeros((RHS, C), F)
                )
                return c

            lax.fori_loop(0, N // C, one_column, 0)
            set_left(False)

        return carry

    lax.fori_loop(0, SLOTS, one_slot, 0)
    turned = near[...].T
    image[...] = start[...] + (turned[:RHS] + turned[RHS:])


def finish_kernel(
    partial, far, residual, direction, image, factors,
    got, mine, first_got, second, second_got,
    send_sem, recv_sem, sum_send, sum_recv,
):
    me = lax.axis_index("dev")
    group, place = me // GROUP, lax.rem(me, GROUP)

    def partner(phase, k):
        if phase == 0:
            return group * GROUP + lax.rem(place + k, GROUP)
        return lax.rem(group + k, GROUP) * GROUP + place

    barrier = pltpu.get_barrier_semaphore()
    for offset in OFFSETS:
        for signed in (offset, -offset):
            pl.semaphore_signal(
                barrier,
                inc=1,
                device_id=(lax.rem(me + signed + DEVS, DEVS),),
                device_id_type=MESH,
            )
    for phase in range(2):
        for k in range(1, GROUP):
            pl.semaphore_signal(
                barrier, inc=1, device_id=(partner(phase, k),), device_id_type=MESH
            )
    pl.semaphore_wait(barrier, 2 * SLOTS + 2 * (GROUP - 1))
    copies = []
    for slot, offset in enumerate(OFFSETS):
        copy = pltpu.make_async_remote_copy(
            src_ref=far.at[slot],
            dst_ref=got.at[slot],
            send_sem=send_sem.at[slot],
            recv_sem=recv_sem.at[slot],
            device_id=(lax.rem(me + offset + DEVS, DEVS),),
            device_id_type=MESH,
        )
        copy.start()
        copies.append(copy)
    r, d = residual[...], direction[...]
    rr = jnp.sum(r * r, axis=1, keepdims=True)
    total = partial[...]
    for slot in range(SLOTS):
        copies[slot].wait()
        total = total + got[slot]
    image[...] = total
    curv = jnp.sum(d * total, axis=1, keepdims=True)
    cross = jnp.sum(r * total, axis=1, keepdims=True)
    square = jnp.sum(total * total, axis=1, keepdims=True)
    lane = lax.broadcasted_iota(jnp.int32, (RHS, 128), 1)
    mine[...] = jnp.where(
        lane == 0, rr, jnp.where(lane == 1, curv, jnp.where(lane == 2, cross, square))
    )

    def exchange(phase, source, slots):
        started = []
        for k in range(1, GROUP):
            copy = pltpu.make_async_remote_copy(
                src_ref=source,
                dst_ref=slots.at[k - 1],
                send_sem=sum_send.at[phase, k - 1],
                recv_sem=sum_recv.at[phase, k - 1],
                device_id=(partner(phase, k),),
                device_id_type=MESH,
            )
            copy.start()
            started.append(copy)
        result = source[...]
        for k, copy in enumerate(started):
            copy.wait()
            result = result + slots[k]
        return result

    second[...] = exchange(0, mine, first_got)
    result = exchange(1, second, second_got)
    rr, curv = result[:, 0:1], result[:, 1:2]
    cross, square = result[:, 2:3], result[:, 3:4]
    alpha = rr / curv
    fresh = jnp.maximum(rr - alpha * (2.0 * cross - alpha * square), 0.0)
    beta = fresh / (rr + 1e-05)
    factors[...] = jnp.where(lane == 0, alpha, beta)


def local(points, noise, pattern, solution, residual, direction):
    vmem = pl.BlockSpec(memory_space=pltpu.VMEM)
    hbm = pl.BlockSpec(memory_space=pl.ANY)
    smem = pl.BlockSpec(memory_space=pltpu.SMEM)
    shape = jax.ShapeDtypeStruct
    work = [
        pltpu.VMEM((N, DEPTH), BF),
        pltpu.VMEM((DEPTH, N), BF),
        pltpu.VMEM((2 * RHS, N), BF),
        pltpu.VMEM((N, 2 * RHS), BF),
        pltpu.VMEM((N, 2 * RHS), F),
        pltpu.VMEM((N, 8), F),
    ]
    dma = pltpu.SemaphoreType.DMA
    got_points, got_dir, start = pl.pallas_call(
        gather_kernel,
        out_shape=(
            shape((SLOTS, DIMS, N), F),
            shape((SLOTS, RHS, N), F),
            shape((RHS, N), F),
        ),
        in_specs=[vmem] * 3,
        out_specs=(hbm, hbm, vmem),
        scratch_shapes=[*work, dma((SLOTS, 2)), dma((SLOTS, 2))],
        compiler_params=pltpu.CompilerParams(
            collective_id=0, has_side_effects=True, vmem_limit_bytes=VMEM_LIMIT
        ),
        name="gather_diagonal",
    )(points, noise.reshape(1, N), direction)
    partial, far = pl.pallas_call(
        pair_kernel,
        out_shape=(shape((RHS, N), F), shape((SLOTS, RHS, N), F)),
        in_specs=[smem] + [vmem] * 5,
        out_specs=(vmem, vmem),
        scratch_shapes=work,
        compiler_params=pltpu.CompilerParams(vmem_limit_bytes=VMEM_LIMIT),
        name="pairs",
    )(pattern, points, direction, got_points, got_dir, start)
    image, factors = pl.pallas_call(
        finish_kernel,
        out_shape=(shape((RHS, N), F), shape((RHS, 128), F)),
        in_specs=[vmem] * 4,
        out_specs=(vmem, vmem),
        scratch_shapes=[
            pltpu.VMEM((SLOTS, RHS, N), F),
            pltpu.VMEM((RHS, 128), F),
            pltpu.VMEM((GROUP - 1, RHS, 128), F),
            pltpu.VMEM((RHS, 128), F),
            pltpu.VMEM((GROUP - 1, RHS, 128), F),
            dma((SLOTS,)),
            dma((SLOTS,)),
            dma((2, GROUP - 1)),
            dma((2, GROUP - 1)),
        ],
        compiler_params=pltpu.CompilerParams(
            collective_id=1, has_side_effects=True, vmem_limit_bytes=VMEM_LIMIT
        ),
        name="finish",
    )(partial, far, residual, direction)
    alpha, beta = factors[:, 0:1], factors[:, 1:2]
    new_solution = solution + alpha * direction
    new_residual = residual - alpha * image
    new_direction = new_residual + beta * direction
    return (new_solution, new_residual, new_direction)


def solution(mesh):
    return jax.shard_map(
        local,
        mesh=mesh,
        in_specs=(
            P(None, "dev"),
            P("dev"),
            P("dev", None),
            P(None, "dev"),
            P(None, "dev"),
            P(None, "dev"),
        ),
        out_specs=(P(None, "dev"), P(None, "dev"), P(None, "dev")),
        check_vma=False,
    )
```

```python
import jax
import jax.numpy as jnp
from jax import lax
from jax.experimental import pallas as pl
from jax.experimental.pallas import tpu as pltpu
from jax.sharding import PartitionSpec as P

F = jnp.float32
BF = jnp.bfloat16
MESH = pl.DeviceIdType.MESH
DIMS = 8
RHS = 16
N = 2048
DEVS = 256
DEPTH = 64
C = 256
VMEM_LIMIT = 56 * 2**20
AXES = ((1, 2), (2, 4), (8, 4), (32, 8))

SLOTS = 4


def split2(x):
    high = x.astype(BF)
    low = (x - high.astype(F)).astype(BF)
    return high.astype(F), low.astype(F)


def split3(x):
    high = x.astype(BF).astype(F)
    rest = x - high
    mid = rest.astype(BF).astype(F)
    low = (rest - mid).astype(BF).astype(F)
    return high, mid, low


def features(points, centre, skip_first):
    row = lax.broadcasted_iota(jnp.int32, points.shape, 0)
    x = jnp.where(row == 0, 0.0 if skip_first else points - centre, points - 0.5)
    norm = jnp.sum(x * x, axis=0, keepdims=True)
    a, b, c = split3(x)
    na, nb, nc = split3(norm)
    ones = jnp.where(row < 3, 1.0, 0.0)
    ones2 = jnp.where((row >= 3) & (row < 6), 1.0, 0.0)
    here = jnp.where(
        row == 0, na, jnp.where(row == 1, nb, jnp.where(row == 2, nc, ones2))
    )
    there = jnp.where(
        row == 3, na, jnp.where(row == 4, nb, jnp.where(row == 5, nc, ones))
    )
    zero = jnp.zeros_like(x)
    left = jnp.concatenate([a, a, b, b, a, c, here, zero], axis=0)
    right = jnp.concatenate(
        [-2.0 * a, -2.0 * b, -2.0 * a, -2.0 * b, -2.0 * c, -2.0 * a, there, zero],
        axis=0,
    )
    return left, right


def middle(first):
    least = jnp.min(first, axis=1, keepdims=True)
    most = jnp.max(first, axis=1, keepdims=True)
    return 0.5 * least + 0.5 * most


def halves_of_rows(direction):
    return jnp.concatenate(split2(direction * 7.0), axis=0)


def kern(dist_sq):
    u = jnp.minimum(jnp.maximum(dist_sq, 1e-30), 1.0)
    s = u * lax.rsqrt(u)
    t = 1.0 - s
    t2 = t * t
    return ((t2 * t2) * t2) * (t * (8.0 / 7.0 - t))


def halves(v):
    high = v.astype(BF)
    low = (v - high.astype(F)).astype(BF)
    return high, low


def dot(a, b):
    return jnp.dot(a, b, preferred_element_type=F)


def dot_t(a, b):
    return lax.dot_general(a, b, (((1,), (1,)), ((), ())), preferred_element_type=F)


def step(me, by):
    return lax.rem(me + by + DEVS, DEVS)


def visit_routes(me):
    p = lax.rem(me, 2)
    comes_from = (2, 4, -3 - 2 * p, -5 - 2 * p)
    goes_to = (-2, -4, 5 - 2 * p, 7 - 2 * p)
    return p, [step(me, x) for x in comes_from], [step(me, x) for x in goes_to]


def greet(barrier, targets):
    for target in targets:
        pl.semaphore_signal(barrier, inc=1, device_id=(target,), device_id_type=MESH)


def greet_neighbours(barrier, me):
    p, comes_from, goes_to = visit_routes(me)
    greet(barrier, [me + 1 - 2 * p])
    for slot in (0, 2, 3):
        greet(barrier, [comes_from[slot], goes_to[slot]])

    @pl.when(p == 0)
    def _():
        greet(barrier, [comes_from[1], goes_to[1]])

    return 9 - 2 * p


def on_slot(slot, p, act):
    if slot == 1:
        pl.when(p == 0)(act)
    else:
        act()


def gather_kernel(
    points_hbm, noise, direction_hbm,
    got_points, got_dir, other_points, other_dir, left2, rows2, image,
    points, direction, left, right, cols, near, column,
    send_sem, recv_sem, local_sem,
):
    me = lax.axis_index("dev")
    p, comes_from, goes_to = visit_routes(me)
    barrier = pltpu.get_barrier_semaphore()
    count = greet_neighbours(barrier, me)
    load_points = pltpu.make_async_copy(points_hbm, points, local_sem.at[0])
    load_dir = pltpu.make_async_copy(direction_hbm, direction, local_sem.at[1])
    load_points.start()
    load_dir.start()
    pl.semaphore_wait(barrier, count)

    def remote(src, dst, slot, part, to):
        return pltpu.make_async_remote_copy(
            src_ref=src,
            dst_ref=dst,
            send_sem=send_sem.at[slot, part],
            recv_sem=recv_sem.at[slot, part],
            device_id=(to,),
            device_id_type=MESH,
        )

    mate = [
        remote(points_hbm, other_points, SLOTS, 0, me + 1 - 2 * p),
        remote(direction_hbm, other_dir, SLOTS, 1, me + 1 - 2 * p),
    ]
    visits = [
        [
            remote(points_hbm, got_points.at[slot], slot, 0, goes_to[slot]),
            remote(direction_hbm, got_dir.at[slot], slot, 1, goes_to[slot]),
        ]
        for slot in range(SLOTS)
    ]
    for copy in mate:
        copy.start()
    for slot in (2, 3, 1, 0):

        def start(slot=slot):
            for copy in visits[slot]:
                copy.start()

        on_slot(slot, p, start)

    load_points.wait()
    load_dir.wait()
    own = points[...]
    a, b = features(own, 0.0, True)
    left[...] = a.T.astype(BF)
    right[...] = b.astype(BF)
    both = halves_of_rows(direction[...])
    rows2[0] = both.astype(BF)
    cols[...] = both.T.astype(BF)
    column[...] = jnp.broadcast_to(points[0:1, :], (8, N)).T
    near[...] = jnp.zeros_like(near)
    image[...] = noise[...] * direction[...]
    a, _ = features(own, middle(points[0:1, :]), False)
    left2[0] = a.T.astype(BF)

    def square(at_row, at_col):
        d = dot(left[at_row, :], right[:, at_col])
        x = column[at_row, 0:1] - points[0:1, at_col]
        high, low = halves(kern(d + x * x))
        w = cols[at_col, :]
        near[at_row, :] += dot(high, w) + dot(low, w)
        return high, low

    def one_column(j, carry):
        at_col = pl.ds(pl.multiple_of(j * C, C), C)

        def one_row(i, acc):
            at_row = pl.ds(pl.multiple_of(i * C, C), C)
            high, low = square(at_row, at_col)
            mine = rows2[0, :, at_row]
            return acc + dot(mine, high) + dot(mine, low)

        far = lax.fori_loop(0, j, one_row, jnp.zeros((2 * RHS, C), F))
        square(at_col, at_col)
        image[:, at_col] += far[:RHS] + far[RHS:]
        return carry

    lax.fori_loop(0, N // C, one_column, 0)
    turned = near[...].T
    image[...] += turned[:RHS] + turned[RHS:]
    for copy in mate:
        copy.wait()
    a, _ = features(other_points[...], middle(other_points[0:1, :]), False)
    left2[1] = a.T.astype(BF)
    rows2[1] = halves_of_rows(other_dir[...]).astype(BF)
    for slot in range(SLOTS):

        def finish(slot=slot):
            for copy in visits[slot]:
                copy.wait()

        on_slot(slot, p, finish)


def pair_kernel(
    core, pattern, points, got_points, got_dir, other_points, other_dir, left2, rows2,
    start, image, other_image, far_out,
    right, cols, near, near_t, left, column, vis_points, vis_rows,
):
    p = core[0]
    near[...] = jnp.zeros_like(near)
    near_t[...] = jnp.zeros_like(near_t)
    far_out[...] = jnp.zeros_like(far_out)

    def one_pair(k, carry):
        slot, which = k // 2, lax.rem(k, 2)
        met_own = (slot == 0) | ((slot < 3) & (p == 1)) | ((slot == 3) & (p == 0))
        met_other = (slot != 1) | (p == 0)
        own_flag = (slot != 0) | (pattern[0, 1] > 0)
        allowed = ((which == 0) & met_own & own_flag) | ((which == 1) & met_other)

        @pl.when(allowed)
        def _():
            mate = (slot == 1) & (p == 1)
            visitor = jnp.where(mate, other_points[...], got_points[slot])
            host = jnp.where(which == 0, points[...], other_points[...])
            theirs, mine = visitor[0:1, :], host[0:1, :]
            low, high = jnp.min(theirs), jnp.max(theirs)
            least, most = jnp.min(mine), jnp.max(mine)
            centre = middle(mine)
            centre_s = 0.5 * least + 0.5 * most
            touch = (low - most < 1.0) & (least - high < 1.0)
            reach = jnp.maximum(
                jnp.maximum(high - centre_s, centre_s - low), most - least
            )
            narrow = reach <= 1.5

            @pl.when(touch)
            def _():
                vis_points[...] = visitor
                both = halves_of_rows(jnp.where(mate, other_dir[...], got_dir[slot]))
                vis_rows[...] = both.astype(BF)
                cols[...] = both.T.astype(BF)

            @pl.when(touch & narrow)
            def _():
                _, b = features(vis_points[...], centre, False)
                right[...] = b.astype(BF)

                def one_column(j, c):
                    at_col = pl.ds(pl.multiple_of(j * C, C), C)
                    d = dot(left2[which], right[:, at_col])
                    high, low = halves(kern(d))
                    near[which] += dot(high, cols[at_col, :])
                    near_t[which] += dot_t(vis_rows[:, at_col], low)
                    mine = rows2[which]
                    far = dot(mine, high) + dot(mine, low)
                    far_out[slot, :, at_col] += far[:RHS] + far[RHS:]
                    return c

                lax.fori_loop(0, N // C, one_column, 0, unroll=True)

            @pl.when(touch & jnp.logical_not(narrow))
            def _():
                a, _ = features(host, centre, True)
                left[...] = a.T.astype(BF)
                column[...] = jnp.broadcast_to(mine, (8, N)).T
                _, b = features(vis_points[...], centre, True)
                right[...] = b.astype(BF)

                def one_column(j, c):
                    at_col = pl.ds(pl.multiple_of(j * C, C), C)

                    def one_row(i, acc):
                        at_row = pl.ds(pl.multiple_of(i * C, C), C)
                        d = dot(left[at_row, :], right[:, at_col])
                        x = column[at_row, 0:1] - vis_points[0:1, at_col]
                        high, low = halves(kern(d + x * x))
                        w = cols[at_col, :]
                        near[which, at_row, :] += dot(high, w) + dot(low, w)
                        rows = rows2[which, :, at_row]
                        return acc + dot(rows, high) + dot(rows, low)

                    far = lax.fori_loop(
                        0, N // C, one_row, jnp.zeros((2 * RHS, C), F)
                    )
                    far_out[slot, :, at_col] += far[:RHS] + far[RHS:]
                    return c

                lax.fori_loop(0, N // C, one_column, 0)

        return carry

    lax.fori_loop(0, 2 * SLOTS, one_pair, 0)

    def total(which):
        turned = near[which].T + near_t[which]
        return turned[:RHS] + turned[RHS:]

    image[...] = start[...] + total(0)
    other_image[...] = total(1) + jnp.where(p == 1, far_out[1], 0.0)


def finish_kernel(
    partial, other_image, far, residual, direction, image, factors,
    got, sums, sum_got,
    send_sem, recv_sem, sum_send, sum_recv,
):
    me = lax.axis_index("dev")
    p, comes_from, goes_to = visit_routes(me)

    def partner(axis, k):
        stride, size = AXES[axis]
        at = lax.rem(me // stride, size)
        return me + (lax.rem(at + k, size) - at) * stride

    barrier = pltpu.get_barrier_semaphore()
    count = greet_neighbours(barrier, me)
    for axis, (_, size) in enumerate(AXES):
        greet(barrier, [partner(axis, k) for k in range(1, size)])
        count = count + (size - 1)
    pl.semaphore_wait(barrier, count)

    def remote(src, slot, to):
        return pltpu.make_async_remote_copy(
            src_ref=src,
            dst_ref=got.at[slot],
            send_sem=send_sem.at[slot],
            recv_sem=recv_sem.at[slot],
            device_id=(to,),
            device_id_type=MESH,
        )

    returns = [remote(far.at[slot], slot, comes_from[slot]) for slot in range(SLOTS)]
    mate = remote(other_image, SLOTS, me + 1 - 2 * p)
    for slot in (2, 3, 1, 0):
        on_slot(slot, p, returns[slot].start)
    mate.start()
    r, d = residual[...], direction[...]
    rr = jnp.sum(r * r, axis=1, keepdims=True)
    mate.wait()
    image[...] = partial[...] + got[SLOTS]
    for slot in (0, 1, 2, 3):

        def add(slot=slot):
            returns[slot].wait()
            image[...] += got[slot]

        on_slot(slot, p, add)
    total = image[...]
    curv = jnp.sum(d * total, axis=1, keepdims=True)
    cross = jnp.sum(r * total, axis=1, keepdims=True)
    square = jnp.sum(total * total, axis=1, keepdims=True)
    lane = lax.broadcasted_iota(jnp.int32, (RHS, 128), 1)
    sums[0] = jnp.where(
        lane == 0, rr, jnp.where(lane == 1, curv, jnp.where(lane == 2, cross, square))
    )
    at = 0
    for axis, (_, size) in enumerate(AXES):
        started = []
        for k in range(1, size):
            copy = pltpu.make_async_remote_copy(
                src_ref=sums.at[axis],
                dst_ref=sum_got.at[at],
                send_sem=sum_send.at[at],
                recv_sem=sum_recv.at[at],
                device_id=(partner(axis, k),),
                device_id_type=MESH,
            )
            copy.start()
            started.append((copy, at))
            at += 1
        acc = sums[axis]
        for copy, place in started:
            copy.wait()
            acc = acc + sum_got[place]
        sums[axis + 1] = acc
    result = sums[len(AXES)]
    rr, curv = result[:, 0:1], result[:, 1:2]
    cross, square = result[:, 2:3], result[:, 3:4]
    alpha = rr / curv
    fresh = jnp.maximum(rr - alpha * (2.0 * cross - alpha * square), 0.0)
    beta = fresh / (rr + 1e-05)
    factors[...] = jnp.where(lane == 0, alpha, beta)


def local(points, noise, pattern, solution, residual, direction):
    vmem = pl.BlockSpec(memory_space=pltpu.VMEM)
    hbm = pl.BlockSpec(memory_space=pl.ANY)
    smem = pl.BlockSpec(memory_space=pltpu.SMEM)
    shape = jax.ShapeDtypeStruct
    dma = pltpu.SemaphoreType.DMA
    got_points, got_dir, other_points, other_dir, left2, rows2, start = pl.pallas_call(
        gather_kernel,
        out_shape=(
            shape((SLOTS, DIMS, N), F),
            shape((SLOTS, RHS, N), F),
            shape((DIMS, N), F),
            shape((RHS, N), F),
            shape((2, N, DEPTH), BF),
            shape((2, 2 * RHS, N), BF),
            shape((RHS, N), F),
        ),
        in_specs=[hbm, vmem, hbm],
        out_specs=(hbm, hbm, vmem, vmem, vmem, vmem, vmem),
        scratch_shapes=[
            pltpu.VMEM((DIMS, N), F),
            pltpu.VMEM((RHS, N), F),
            pltpu.VMEM((N, DEPTH), BF),
            pltpu.VMEM((DEPTH, N), BF),
            pltpu.VMEM((N, 2 * RHS), BF),
            pltpu.VMEM((N, 2 * RHS), F),
            pltpu.VMEM((N, 8), F),
            dma((SLOTS + 1, 2)),
            dma((SLOTS + 1, 2)),
            dma((2,)),
        ],
        compiler_params=pltpu.CompilerParams(
            collective_id=0, has_side_effects=True, vmem_limit_bytes=VMEM_LIMIT
        ),
        name="gather_diagonal",
    )(points, noise.reshape(1, N), direction)
    core = lax.rem(lax.axis_index("dev"), 2).reshape(1).astype(jnp.int32)
    partial, other_image, far = pl.pallas_call(
        pair_kernel,
        out_shape=(
            shape((RHS, N), F),
            shape((RHS, N), F),
            shape((SLOTS, RHS, N), F),
        ),
        in_specs=[smem] * 2 + [vmem] * 8,
        out_specs=(vmem, vmem, vmem),
        scratch_shapes=[
            pltpu.VMEM((DEPTH, N), BF),
            pltpu.VMEM((N, 2 * RHS), BF),
            pltpu.VMEM((2, N, 2 * RHS), F),
            pltpu.VMEM((2, 2 * RHS, N), F),
            pltpu.VMEM((N, DEPTH), BF),
            pltpu.VMEM((N, 8), F),
            pltpu.VMEM((DIMS, N), F),
            pltpu.VMEM((2 * RHS, N), BF),
        ],
        compiler_params=pltpu.CompilerParams(vmem_limit_bytes=VMEM_LIMIT),
        name="pairs",
    )(
        core, pattern, points, got_points, got_dir, other_points, other_dir, left2,
        rows2, start,
    )
    exchanges = sum(size - 1 for _, size in AXES)
    image, factors = pl.pallas_call(
        finish_kernel,
        out_shape=(shape((RHS, N), F), shape((RHS, 128), F)),
        in_specs=[vmem] * 5,
        out_specs=(vmem, vmem),
        scratch_shapes=[
            pltpu.VMEM((SLOTS + 1, RHS, N), F),
            pltpu.VMEM((len(AXES) + 1, RHS, 128), F),
            pltpu.VMEM((exchanges, RHS, 128), F),
            dma((SLOTS + 1,)),
            dma((SLOTS + 1,)),
            dma((exchanges,)),
            dma((exchanges,)),
        ],
        compiler_params=pltpu.CompilerParams(
            collective_id=1, has_side_effects=True, vmem_limit_bytes=VMEM_LIMIT
        ),
        name="finish",
    )(partial, other_image, far, residual, direction)
    alpha, beta = factors[:, 0:1], factors[:, 1:2]
    new_solution = solution + alpha * direction
    new_residual = residual - alpha * image
    new_direction = new_residual + beta * direction
    return (new_solution, new_residual, new_direction)


def solution(mesh):
    return jax.shard_map(
        local,
        mesh=mesh,
        in_specs=(
            P(None, "dev"),
            P("dev"),
            P("dev", None),
            P(None, "dev"),
            P(None, "dev"),
            P(None, "dev"),
        ),
        out_specs=(P(None, "dev"), P(None, "dev"), P(None, "dev")),
        check_vma=False,
    )
```

```python
import jax
import jax.numpy as jnp
from jax import lax
from jax.experimental import pallas as pl
from jax.experimental.pallas import tpu as pltpu
from jax.sharding import PartitionSpec as P

F = jnp.float32
BF = jnp.bfloat16
MESH = pl.DeviceIdType.MESH
DIMS = 8
RHS = 16
N = 2048
DEVS = 256
DEPTH = 64
C = 256
VMEM_LIMIT = 56 * 2**20
AXES = ((1, 2), (2, 4), (8, 4), (32, 8))

SLOTS = 4
LATE = ((1, 0), (1, 1), (2, 0), (2, 1))
NARROW = 1.5


def split2(x):
    high = x.astype(BF)
    low = (x - high.astype(F)).astype(BF)
    return high.astype(F), low.astype(F)


def split3(x):
    high = x.astype(BF).astype(F)
    rest = x - high
    mid = rest.astype(BF).astype(F)
    low = (rest - mid).astype(BF).astype(F)
    return high, mid, low


def features(points, centre, skip_first):
    row = lax.broadcasted_iota(jnp.int32, points.shape, 0)
    x = jnp.where(row == 0, 0.0 if skip_first else points - centre, points - 0.5)
    norm = jnp.sum(x * x, axis=0, keepdims=True)
    a, b, c = split3(x)
    na, nb, nc = split3(norm)
    ones = jnp.where(row < 3, 1.0, 0.0)
    ones2 = jnp.where((row >= 3) & (row < 6), 1.0, 0.0)
    here = jnp.where(
        row == 0, na, jnp.where(row == 1, nb, jnp.where(row == 2, nc, ones2))
    )
    there = jnp.where(
        row == 3, na, jnp.where(row == 4, nb, jnp.where(row == 5, nc, ones))
    )
    zero = jnp.zeros_like(x)
    left = jnp.concatenate([a, a, b, b, a, c, here, zero], axis=0)
    right = jnp.concatenate(
        [-2.0 * a, -2.0 * b, -2.0 * a, -2.0 * b, -2.0 * c, -2.0 * a, there, zero],
        axis=0,
    )
    return left, right


def middle(first):
    least = jnp.min(first, axis=1, keepdims=True)
    most = jnp.max(first, axis=1, keepdims=True)
    return 0.5 * least + 0.5 * most


def halves_of_rows(direction):
    return jnp.concatenate(split2(direction * 7.0), axis=0)


def kern(dist_sq):
    u = jnp.minimum(jnp.maximum(dist_sq, 1e-30), 1.0)
    s = u * lax.rsqrt(u)
    t = 1.0 - s
    t2 = t * t
    return ((t2 * t2) * t2) * (t * (8.0 / 7.0 - t))


def halves(v):
    high = v.astype(BF)
    low = (v - high.astype(F)).astype(BF)
    return high, low


def fold(both):
    return both[:RHS] + both[RHS:]


def dot(a, b):
    return jnp.dot(a, b, preferred_element_type=F)


def dot_t(a, b):
    return lax.dot_general(a, b, (((1,), (1,)), ((), ())), preferred_element_type=F)


def apart(host, visitor):
    least, most = (f(host, axis=1, keepdims=True) for f in (jnp.min, jnp.max))
    low, high = (f(visitor, axis=1, keepdims=True) for f in (jnp.min, jnp.max))
    centre = 0.5 * least + 0.5 * most
    reach = jnp.maximum(jnp.maximum(high - centre, centre - low), most - least)
    touch = (low - most < 1.0) & (least - high < 1.0)
    return jnp.where(touch & (reach <= NARROW), 1.0, 0.0)


def choose(flag, value, other):
    return jnp.where(jnp.broadcast_to(flag, value.shape) > 0.0, value, other)


def met(slot, which, p):
    if which == 0:
        return (1.0, p, p, 1.0 - p)[slot]
    return (1.0, 1.0 - p, 1.0, 1.0)[slot]


def pick(flags):
    taken, picked = 0.0, []
    for flag in flags:
        here = flag * (1.0 - taken)
        taken = taken + here
        picked.append(here)
    return picked


def one_tile(host, host_dir, visitor, visitor_dir, left, right, cols, rows, vis_rows, near, near_t, far):
    centre = middle(host[0:1, :])
    a, _ = features(host, centre, False)
    left[...] = a.T.astype(BF)
    _, b = features(visitor, centre, False)
    right[...] = b.astype(BF)
    rows[...] = halves_of_rows(host_dir).astype(BF)
    both = halves_of_rows(visitor_dir)
    vis_rows[...] = both.astype(BF)
    cols[...] = both.T.astype(BF)
    near[...] = jnp.zeros_like(near)
    near_t[...] = jnp.zeros_like(near_t)
    for j in range(N // C):
        at_col = slice(j * C, (j + 1) * C)
        high, low = halves(kern(dot(left[...], right[:, at_col])))
        near[...] += dot(high, cols[at_col, :])
        near_t[...] += dot_t(vis_rows[:, at_col], low)
        far[:, at_col] = fold(dot(rows[...], high) + dot(rows[...], low))


def visit_routes(me):
    p = lax.rem(me, 2)

    def route(slot, by):
        there = me + by
        used = (there >= 0) & (there < DEVS)
        if slot == 1:
            used = used & (p == 0)
        return lax.rem(there + DEVS, DEVS), used

    comes_from = [route(i, by) for i, by in enumerate((2, 4, -3 - 2 * p, -5 - 2 * p))]
    goes_to = [route(i, by) for i, by in enumerate((-2, -4, 5 - 2 * p, 7 - 2 * p))]
    return p, comes_from, goes_to


def greet(barrier, targets):
    for target in targets:
        pl.semaphore_signal(barrier, inc=1, device_id=(target,), device_id_type=MESH)


def greet_neighbours(barrier, me):
    p, comes_from, goes_to = visit_routes(me)
    greet(barrier, [me + 1 - 2 * p])
    count = 1
    for device, used in comes_from + goes_to:

        @pl.when(used)
        def _(device=device):
            greet(barrier, [device])

        count = count + jnp.where(used, 1, 0)
    return count


def gather_kernel(
    points_hbm, noise, direction_hbm,
    got_points, got_dir, other_points, other_dir, left2, rows2, image, other_image,
    far_first, code,
    points, direction, left, right, cols, near, column, rows, vis_rows, near_t, far_now,
    send_sem, recv_sem, local_sem,
):
    me = lax.axis_index("dev")
    p, comes_from, goes_to = visit_routes(me)
    barrier = pltpu.get_barrier_semaphore()
    count = greet_neighbours(barrier, me)
    load_points = pltpu.make_async_copy(points_hbm, points, local_sem.at[0])
    load_dir = pltpu.make_async_copy(direction_hbm, direction, local_sem.at[1])
    load_points.start()
    load_dir.start()
    pl.semaphore_wait(barrier, count)

    def remote(src, dst, slot, part, to):
        return pltpu.make_async_remote_copy(
            src_ref=src,
            dst_ref=dst,
            send_sem=send_sem.at[slot, part],
            recv_sem=recv_sem.at[slot, part],
            device_id=(to,),
            device_id_type=MESH,
        )

    mate = [
        remote(points_hbm, other_points, SLOTS, 0, me + 1 - 2 * p),
        remote(direction_hbm, other_dir, SLOTS, 1, me + 1 - 2 * p),
    ]
    visits = [
        [
            remote(points_hbm, got_points.at[slot], slot, 0, goes_to[slot][0]),
            remote(direction_hbm, got_dir.at[slot], slot, 1, goes_to[slot][0]),
        ]
        for slot in range(SLOTS)
    ]
    for copy in mate:
        copy.start()

    def send(slot):
        @pl.when(goes_to[slot][1])
        def _():
            for copy in visits[slot]:
                copy.start()

    def receive(slot):
        @pl.when(comes_from[slot][1])
        def _():
            for copy in visits[slot]:
                copy.wait_recv()

        @pl.when(jnp.logical_not(comes_from[slot][1]))
        def _():
            got_points[slot] = other_points[...]
            got_dir[slot] = other_dir[...]

    send(0)
    send(3)
    load_points.wait()
    load_dir.wait()
    own = points[...]
    a, b = features(own, 0.0, True)
    left[...] = a.T.astype(BF)
    right[...] = b.astype(BF)
    both = halves_of_rows(direction[...])
    rows2[0] = both.astype(BF)
    cols[...] = both.T.astype(BF)
    column[...] = jnp.broadcast_to(points[0:1, :], (128, N)).T
    near[...] = jnp.zeros_like(near)
    image[...] = noise[...] * direction[...]
    a, _ = features(own, middle(points[0:1, :]), False)
    left2[0] = a.T.astype(BF)

    for j in range(N // C):
        at_col, size = slice(j * C, (j + 1) * C), (j + 1) * C
        d = dot(left[:size, :], right[:, at_col])
        x = jnp.concatenate([column[:size, :]] * (C // 128), axis=1)
        x = x - points[0:1, at_col]
        high, low = halves(kern(d + x * x))
        near[:size, :] += dot(high, cols[at_col, :])
        image[:, :size] += fold(dot_t(rows2[0, :, at_col], low))
        if j:
            mine = rows2[0, :, : j * C]
            far = dot(mine, high[: j * C]) + dot(mine, low[: j * C])
            image[:, at_col] += fold(far)
    image[...] += fold(near[...].T)
    for copy in mate:
        copy.wait()
    receive(0)
    receive(3)
    send(2)
    send(1)

    other = other_points[...]
    a, _ = features(other, middle(other[0:1, :]), False)
    left2[1] = a.T.astype(BF)
    rows2[1] = halves_of_rows(other_dir[...]).astype(BF)

    pf = p.astype(F)
    hosts = (points, other_points)
    early = [(0, 0), (0, 1), (3, 0), (3, 1), (1, 0)]
    flags = []
    for slot, which in early:
        visitor = other_points if slot == 1 else got_points.at[slot]
        here = jnp.where(comes_from[slot][1], 1.0, 0.0)
        may = pf if slot == 1 else met(slot, which, pf) * here
        flags.append(apart(hosts[which][0:1, :], visitor[0:1, :]) * may)
    picked = pick(flags)
    of_slot = {0: picked[0] + picked[1], 1: picked[4], 3: picked[2] + picked[3]}
    of_other = picked[1] + picked[3]
    visitor = choose(of_slot[1], other, got_points[0])
    visitor = choose(of_slot[3], got_points[3], visitor)
    visitor_dir = choose(of_slot[1], other_dir[...], got_dir[0])
    visitor_dir = choose(of_slot[3], got_dir[3], visitor_dir)
    host = choose(of_other, other, own)
    host_dir = choose(of_other, other_dir[...], direction[...])
    one_tile(
        host, host_dir, visitor, visitor_dir,
        left, right, cols, rows, vis_rows, near, near_t, far_now,
    )
    result = fold(near[...].T + near_t[...])
    of_own = picked[0] + picked[2] + picked[4]
    image[...] += choose(of_own, result, jnp.zeros_like(result))
    other_image[...] = choose(of_other, result, jnp.zeros_like(result))
    for slot in range(SLOTS):
        if slot in of_slot:
            far_first[slot] = choose(of_slot[slot], far_now[...], jnp.zeros_like(result))
        else:
            far_first[slot] = jnp.zeros_like(result)
    receive(2)
    receive(1)

    flags = []
    for slot, which in LATE:
        if (slot, which) == (1, 0):
            may = pf * (1.0 - picked[4])
        else:
            may = met(slot, which, pf) * jnp.where(comes_from[slot][1], 1.0, 0.0)
        flag = apart(hosts[which][0:1, :], got_points[slot, 0:1, :])
        flags.append(flag * may)
    late = pick(flags)
    code[...] = jnp.zeros_like(code)
    for (slot, which), here in zip(early, picked, strict=True):
        at = 2 * slot + which
        code[at : at + 1, :] += jnp.broadcast_to(here, (1, 128))
    for (slot, which), here in zip(LATE, late, strict=True):
        at = 2 * slot + which
        code[at : at + 1, :] += jnp.broadcast_to(2.0 * here, (1, 128))
    for slot in range(SLOTS):

        @pl.when(goes_to[slot][1])
        def _(slot=slot):
            for copy in visits[slot]:
                copy.wait_send()


def pair_kernel(
    place, pattern, code, points, got_points, got_dir, other_points, left2, rows2,
    start, other_start, far_first, image, other_image, far_out,
    right, cols, near, near_t, left, column, vis_points, vis_rows, extent,
):
    me = place[0]
    p = lax.rem(me, 2)
    firsts = [points[0:1, :], other_points[0:1, :]]
    firsts += [got_points[slot, 0:1, :] for slot in range(SLOTS)]
    for at, first in enumerate(firsts):
        extent[at, 0] = jnp.min(first)
        extent[at, 1] = jnp.max(first)
    near[...] = jnp.zeros_like(near)
    near_t[...] = jnp.zeros_like(near_t)
    far_out[...] = far_first[...]

    def one_pair(k, carry):
        slot, which = k // 2, lax.rem(k, 2)
        met_own = (slot == 0) | ((slot < 3) & (p == 1)) | ((slot == 3) & (p == 0))
        met_other = (slot != 1) | (p == 0)
        own_flag = (slot != 0) | (pattern[0, 1] > 0)
        ahead = me + jnp.where(slot == 0, 2, 4)
        behind = me - 2 * p - jnp.where(slot == 2, 3, 5)
        inside = ((slot == 1) & (p == 1)) | ((slot < 2) & (ahead < DEVS))
        inside = inside | ((slot >= 2) & (behind >= 0))
        allowed = ((which == 0) & met_own & own_flag) | ((which == 1) & met_other)
        allowed = allowed & inside

        theirs = slot + 2
        low, high = extent[theirs, 0], extent[theirs, 1]
        least, most = extent[which, 0], extent[which, 1]
        centre_s = 0.5 * least + 0.5 * most
        touch = (low - most < 1.0) & (least - high < 1.0)
        reach = jnp.maximum(jnp.maximum(high - centre_s, centre_s - low), most - least)
        narrow = reach <= NARROW
        left_over = code[k, 0] < 0.5

        @pl.when(allowed & touch & left_over)
        def _():
            visitor = got_points[slot]
            host = jnp.where(which == 0, points[...], other_points[...])
            mine = host[0:1, :]
            centre = middle(mine)
            vis_points[...] = visitor
            both = halves_of_rows(got_dir[slot])
            vis_rows[...] = both.astype(BF)
            cols[...] = both.T.astype(BF)

            @pl.when(narrow)
            def _():
                _, b = features(vis_points[...], centre, False)
                right[...] = b.astype(BF)

                def one_column(j, c):
                    at_col = pl.ds(pl.multiple_of(j * C, C), C)
                    d = dot(left2[which], right[:, at_col])
                    high, low = halves(kern(d))
                    near[which] += dot(high, cols[at_col, :])
                    near_t[which] += dot_t(vis_rows[:, at_col], low)
                    mine = rows2[which]
                    far = dot(mine, high) + dot(mine, low)
                    far_out[slot, :, at_col] += fold(far)
                    return c

                lax.fori_loop(0, N // C, one_column, 0, unroll=True)

            @pl.when(jnp.logical_not(narrow))
            def _():
                a, _ = features(host, centre, True)
                left[...] = a.T.astype(BF)
                column[...] = jnp.broadcast_to(mine, (8, N)).T
                _, b = features(vis_points[...], centre, True)
                right[...] = b.astype(BF)

                def one_column(j, c):
                    at_col = pl.ds(pl.multiple_of(j * C, C), C)

                    def one_row(i, acc):
                        at_row = pl.ds(pl.multiple_of(i * C, C), C)
                        d = dot(left[at_row, :], right[:, at_col])
                        x = column[at_row, 0:1] - vis_points[0:1, at_col]
                        high, low = halves(kern(d + x * x))
                        w = cols[at_col, :]
                        near[which, at_row, :] += dot(high, w) + dot(low, w)
                        rows = rows2[which, :, at_row]
                        return acc + dot(rows, high) + dot(rows, low)

                    far = lax.fori_loop(
                        0, N // C, one_row, jnp.zeros((2 * RHS, C), F)
                    )
                    far_out[slot, :, at_col] += fold(far)
                    return c

                lax.fori_loop(0, N // C, one_column, 0)

        return carry

    lax.fori_loop(0, 2 * SLOTS, one_pair, 0)

    def total(which):
        return fold(near[which].T + near_t[which])

    image[...] = start[...] + total(0)
    other_image[...] = other_start[...] + total(1)


def finish_kernel(
    partial, other_partial, far, residual, direction, code, points, got_points, got_dir,
    other_points, other_dir, image, factors,
    got, sums, sum_got, other_image, far_last,
    left, right, cols, rows, vis_rows, near, near_t, far_now,
    send_sem, recv_sem, sum_send, sum_recv,
):
    me = lax.axis_index("dev")
    p, comes_from, goes_to = visit_routes(me)

    def partner(axis, k):
        stride, size = AXES[axis]
        at = lax.rem(me // stride, size)
        return me + (lax.rem(at + k, size) - at) * stride

    barrier = pltpu.get_barrier_semaphore()
    count = greet_neighbours(barrier, me)
    for axis, (_, size) in enumerate(AXES):
        greet(barrier, [partner(axis, k) for k in range(1, size)])
        count = count + (size - 1)
    pl.semaphore_wait(barrier, count)

    def remote(src, slot, to):
        return pltpu.make_async_remote_copy(
            src_ref=src,
            dst_ref=got.at[slot],
            send_sem=send_sem.at[slot],
            recv_sem=recv_sem.at[slot],
            device_id=(to,),
            device_id_type=MESH,
        )

    returns = [
        remote(far_last.at[slot - 1] if slot in (1, 2) else far.at[slot], slot, to)
        for slot, (to, _) in enumerate(comes_from)
    ]
    mate = remote(other_image, SLOTS, me + 1 - 2 * p)

    def send(slot):
        pl.when(comes_from[slot][1])(returns[slot].start)

    send(0)
    send(3)
    r, d = residual[...], direction[...]
    rr = jnp.sum(r * r, axis=1, keepdims=True)

    late = [
        jnp.where(code[2 * slot + which : 2 * slot + which + 1, 0:1] > 1.5, 1.0, 0.0)
        for slot, which in LATE
    ]
    of_slot = {1: late[0] + late[1], 2: late[2] + late[3]}
    of_own, of_other = late[0] + late[2], late[1] + late[3]
    one_tile(
        choose(of_other, other_points[...], points[...]),
        choose(of_other, other_dir[...], d),
        choose(of_slot[1], got_points[1], got_points[2]),
        choose(of_slot[1], got_dir[1], got_dir[2]),
        left, right, cols, rows, vis_rows, near, near_t, far_now,
    )
    result = fold(near[...].T + near_t[...])
    nothing = jnp.zeros_like(result)
    for slot in (1, 2):
        far_last[slot - 1] = far[slot] + choose(of_slot[slot], far_now[...], nothing)
    send(2)
    send(1)
    other = other_partial[...] + choose(of_other, result, nothing)
    other_image[...] = other + jnp.where(p == 1, far_last[0], 0.0)
    mate.start()
    image[...] = partial[...] + choose(of_own, result, nothing)
    mate.wait()
    image[...] += got[SLOTS]
    for slot in (0, 3, 1, 2):

        @pl.when(goes_to[slot][1])
        def _(slot=slot):
            returns[slot].wait_recv()
            image[...] += got[slot]

    total = image[...]
    curv = jnp.sum(d * total, axis=1, keepdims=True)
    cross = jnp.sum(r * total, axis=1, keepdims=True)
    square = jnp.sum(total * total, axis=1, keepdims=True)
    lane = lax.broadcasted_iota(jnp.int32, (RHS, 128), 1)
    sums[0] = jnp.where(
        lane == 0, rr, jnp.where(lane == 1, curv, jnp.where(lane == 2, cross, square))
    )
    at = 0
    leaving = []
    for axis, (_, size) in enumerate(AXES):
        started = []
        for k in range(1, size):
            copy = pltpu.make_async_remote_copy(
                src_ref=sums.at[axis],
                dst_ref=sum_got.at[at],
                send_sem=sum_send.at[at],
                recv_sem=sum_recv.at[at],
                device_id=(partner(axis, k),),
                device_id_type=MESH,
            )
            copy.start()
            started.append((copy, at))
            at += 1
        acc = sums[axis]
        for copy, place in started:
            copy.wait_recv()
            acc = acc + sum_got[place]
        sums[axis + 1] = acc
        leaving += [copy for copy, _ in started]
    result = sums[len(AXES)]
    rr, curv = result[:, 0:1], result[:, 1:2]
    cross, square = result[:, 2:3], result[:, 3:4]
    alpha = rr / curv
    fresh = jnp.maximum(rr - alpha * (2.0 * cross - alpha * square), 0.0)
    beta = fresh / (rr + 1e-05)
    factors[0] = jnp.broadcast_to(alpha, (RHS, 128))
    factors[1] = jnp.broadcast_to(beta, (RHS, 128))
    for copy in leaving:
        copy.wait_send()
    for slot in range(SLOTS):
        pl.when(comes_from[slot][1])(returns[slot].wait_send)


def update_kernel(
    factors, image, solution, residual, direction, new_solution, new_residual, new_dir
):
    alpha, beta = factors[0, :, 0:1], factors[1, :, 0:1]
    d = direction[...]
    new_solution[...] = solution[...] + alpha * d
    r = residual[...] - alpha * image[...]
    new_residual[...] = r
    new_dir[...] = r + beta * d


def local(points, noise, pattern, solution, residual, direction):
    vmem = pl.BlockSpec(memory_space=pltpu.VMEM)
    hbm = pl.BlockSpec(memory_space=pl.ANY)
    smem = pl.BlockSpec(memory_space=pltpu.SMEM)
    shape = jax.ShapeDtypeStruct
    dma = pltpu.SemaphoreType.DMA
    (
        got_points, got_dir, other_points, other_dir, left2, rows2, start, other_start,
        far_first, code,
    ) = pl.pallas_call(
        gather_kernel,
        out_shape=(
            shape((SLOTS, DIMS, N), F),
            shape((SLOTS, RHS, N), F),
            shape((DIMS, N), F),
            shape((RHS, N), F),
            shape((2, N, DEPTH), BF),
            shape((2, 2 * RHS, N), BF),
            shape((RHS, N), F),
            shape((RHS, N), F),
            shape((SLOTS, RHS, N), F),
            shape((2 * SLOTS, 128), F),
        ),
        in_specs=[hbm, vmem, hbm],
        out_specs=(vmem,) * 10,
        scratch_shapes=[
            pltpu.VMEM((DIMS, N), F),
            pltpu.VMEM((RHS, N), F),
            pltpu.VMEM((N, DEPTH), BF),
            pltpu.VMEM((DEPTH, N), BF),
            pltpu.VMEM((N, 2 * RHS), BF),
            pltpu.VMEM((N, 2 * RHS), F),
            pltpu.VMEM((N, 128), F),
            pltpu.VMEM((2 * RHS, N), BF),
            pltpu.VMEM((2 * RHS, N), BF),
            pltpu.VMEM((2 * RHS, N), F),
            pltpu.VMEM((RHS, N), F),
            dma((SLOTS + 1, 2)),
            dma((SLOTS + 1, 2)),
            dma((2,)),
        ],
        compiler_params=pltpu.CompilerParams(
            collective_id=0, has_side_effects=True, vmem_limit_bytes=VMEM_LIMIT
        ),
        name="gather_diagonal",
    )(points, noise.reshape(1, N), direction)
    place = lax.axis_index("dev").reshape(1).astype(jnp.int32)
    partial, other_image, far = pl.pallas_call(
        pair_kernel,
        out_shape=(
            shape((RHS, N), F),
            shape((RHS, N), F),
            shape((SLOTS, RHS, N), F),
        ),
        in_specs=[smem] * 3 + [vmem] * 9,
        out_specs=(vmem, vmem, vmem),
        scratch_shapes=[
            pltpu.VMEM((DEPTH, N), BF),
            pltpu.VMEM((N, 2 * RHS), BF),
            pltpu.VMEM((2, N, 2 * RHS), F),
            pltpu.VMEM((2, 2 * RHS, N), F),
            pltpu.VMEM((N, DEPTH), BF),
            pltpu.VMEM((N, 8), F),
            pltpu.VMEM((DIMS, N), F),
            pltpu.VMEM((2 * RHS, N), BF),
            pltpu.SMEM((SLOTS + 2, 2), F),
        ],
        compiler_params=pltpu.CompilerParams(vmem_limit_bytes=VMEM_LIMIT),
        name="pairs",
    )(
        place, pattern, code, points, got_points, got_dir, other_points, left2, rows2,
        start, other_start, far_first,
    )
    exchanges = sum(size - 1 for _, size in AXES)
    image, factors = pl.pallas_call(
        finish_kernel,
        out_shape=(shape((RHS, N), F), shape((2, RHS, 128), F)),
        in_specs=[vmem] * 11,
        out_specs=(vmem, vmem),
        scratch_shapes=[
            pltpu.VMEM((SLOTS + 1, RHS, N), F),
            pltpu.VMEM((len(AXES) + 1, RHS, 128), F),
            pltpu.VMEM((exchanges, RHS, 128), F),
            pltpu.VMEM((RHS, N), F),
            pltpu.VMEM((2, RHS, N), F),
            pltpu.VMEM((N, DEPTH), BF),
            pltpu.VMEM((DEPTH, N), BF),
            pltpu.VMEM((N, 2 * RHS), BF),
            pltpu.VMEM((2 * RHS, N), BF),
            pltpu.VMEM((2 * RHS, N), BF),
            pltpu.VMEM((N, 2 * RHS), F),
            pltpu.VMEM((2 * RHS, N), F),
            pltpu.VMEM((RHS, N), F),
            dma((SLOTS + 1,)),
            dma((SLOTS + 1,)),
            dma((exchanges,)),
            dma((exchanges,)),
        ],
        compiler_params=pltpu.CompilerParams(
            collective_id=1, has_side_effects=True, vmem_limit_bytes=VMEM_LIMIT
        ),
        name="finish",
    )(
        partial, other_image, far, residual, direction, code, points, got_points,
        got_dir, other_points, other_dir,
    )
    return pl.pallas_call(
        update_kernel,
        out_shape=(shape((RHS, N), F),) * 3,
        in_specs=[vmem] * 5,
        out_specs=(vmem,) * 3,
        name="update",
    )(factors, image, solution, residual, direction)


def solution(mesh):
    return jax.shard_map(
        local,
        mesh=mesh,
        in_specs=(
            P(None, "dev"),
            P("dev"),
            P("dev", None),
            P(None, "dev"),
            P(None, "dev"),
            P(None, "dev"),
        ),
        out_specs=(P(None, "dev"), P(None, "dev"), P(None, "dev")),
        check_vma=False,
    )
```

```python
import jax
import jax.numpy as jnp
from jax import lax
from jax.experimental import pallas as pl
from jax.experimental.pallas import tpu as pltpu
from jax.sharding import PartitionSpec as P

F = jnp.float32
BF = jnp.bfloat16
MESH = pl.DeviceIdType.MESH
DIMS = 8
RHS = 16
N = 2048
DEVS = 256
DEPTH = 64
C = 256
VMEM_LIMIT = 56 * 2**20
AXES = ((1, 2), (2, 4), (8, 4), (32, 8))

SLOTS = 4
CUT = 6
LATE = ((1, 0), (1, 1), (2, 0), (2, 1))
NARROW = 1.5


def split2(x):
    high = x.astype(BF)
    low = (x - high.astype(F)).astype(BF)
    return high.astype(F), low.astype(F)


def split3(x):
    high = x.astype(BF).astype(F)
    rest = x - high
    mid = rest.astype(BF).astype(F)
    low = (rest - mid).astype(BF).astype(F)
    return high, mid, low


def features(points, centre, skip_first):
    row = lax.broadcasted_iota(jnp.int32, points.shape, 0)
    x = jnp.where(row == 0, 0.0 if skip_first else points - centre, points - 0.5)
    norm = jnp.sum(x * x, axis=0, keepdims=True)
    a, b, c = split3(x)
    na, nb, nc = split3(norm)
    ones = jnp.where(row < 3, 1.0, 0.0)
    ones2 = jnp.where((row >= 3) & (row < 6), 1.0, 0.0)
    here = jnp.where(
        row == 0, na, jnp.where(row == 1, nb, jnp.where(row == 2, nc, ones2))
    )
    there = jnp.where(
        row == 3, na, jnp.where(row == 4, nb, jnp.where(row == 5, nc, ones))
    )
    zero = jnp.zeros_like(x)
    left = jnp.concatenate([a, a, b, b, a, c, here, zero], axis=0)
    right = jnp.concatenate(
        [-2.0 * a, -2.0 * b, -2.0 * a, -2.0 * b, -2.0 * c, -2.0 * a, there, zero],
        axis=0,
    )
    return left, right


def middle(first):
    least = jnp.min(first, axis=1, keepdims=True)
    most = jnp.max(first, axis=1, keepdims=True)
    return 0.5 * least + 0.5 * most


def halves_of_rows(direction):
    return jnp.concatenate(split2(direction * 7.0), axis=0)


def kern(dist_sq):
    u = jnp.minimum(jnp.maximum(dist_sq, 1e-30), 1.0)
    s = u * lax.rsqrt(u)
    t = 1.0 - s
    t2 = t * t
    return ((t2 * t2) * t2) * (t * (8.0 / 7.0 - t))


def halves(v):
    high = v.astype(BF)
    low = (v - high.astype(F)).astype(BF)
    return high, low


def fold(both):
    return both[:RHS] + both[RHS:]


def dot(a, b):
    return jnp.dot(a, b, preferred_element_type=F)


def dot_t(a, b):
    return lax.dot_general(a, b, (((1,), (1,)), ((), ())), preferred_element_type=F)


def extent_of(first):
    return jnp.min(first, axis=1, keepdims=True), jnp.max(first, axis=1, keepdims=True)


def apart(host, visitor):
    (least, most), (low, high) = host, visitor
    centre = 0.5 * least + 0.5 * most
    reach = jnp.maximum(jnp.maximum(high - centre, centre - low), most - least)
    touch = (low - most < 1.0) & (least - high < 1.0)
    return jnp.where(touch & (reach <= NARROW), 1.0, 0.0)


def choose(flag, value, other):
    return jnp.where(jnp.broadcast_to(flag, value.shape) > 0.0, value, other)


def met(slot, which, p):
    if which == 0:
        return (1.0, p, p, 1.0 - p)[slot]
    return (1.0, 1.0 - p, 1.0, 1.0)[slot]


def pick(flags):
    taken, picked = 0.0, []
    for flag in flags:
        here = flag * (1.0 - taken)
        taken = taken + here
        picked.append(here)
    return picked


def set_rows(host_dir, visitor_dir, cols, rows, vis_rows):
    rows[...] = halves_of_rows(host_dir).astype(BF)
    both = halves_of_rows(visitor_dir)
    vis_rows[...] = both.astype(BF)
    cols[...] = both.T.astype(BF)


def one_tile(host, host_dir, visitor, visitor_dir, left, right, cols, rows, vis_rows, near, near_t, far, after=None):
    centre = middle(host[0:1, :])
    a, _ = features(host, centre, False)
    left[...] = a.T.astype(BF)
    _, b = features(visitor, centre, False)
    right[...] = b.astype(BF)
    set_rows(host_dir, visitor_dir, cols, rows, vis_rows)
    for j in range(N // C):
        at_col = slice(j * C, (j + 1) * C)
        high, low = halves(kern(dot(left[...], right[:, at_col])))
        one = dot(high, cols[at_col, :])
        two = dot_t(vis_rows[:, at_col], low)
        near[...] = one if j == 0 else near[...] + one
        near_t[...] = two if j == 0 else near_t[...] + two
        far[:, at_col] = fold(dot(rows[...], high) + dot(rows[...], low))
        if after:
            after(j + 1)
    return fold(near[...].T + near_t[...])


def visit_routes(me):
    p = lax.rem(me, 2)

    def route(slot, by):
        there = me + by
        used = (there >= 0) & (there < DEVS)
        if slot == 1:
            used = used & (p == 0)
        return lax.rem(there + DEVS, DEVS), used

    comes_from = [route(i, by) for i, by in enumerate((2, 4, -3 - 2 * p, -5 - 2 * p))]
    goes_to = [route(i, by) for i, by in enumerate((-2, -4, 5 - 2 * p, 7 - 2 * p))]
    return p, comes_from, goes_to


def greet(barrier, targets):
    for target in targets:
        pl.semaphore_signal(barrier, inc=1, device_id=(target,), device_id_type=MESH)


def greet_neighbours(barrier, me):
    p, comes_from, goes_to = visit_routes(me)
    greet(barrier, [me + 1 - 2 * p])
    count = 1
    for device, used in comes_from + goes_to:

        @pl.when(used)
        def _(device=device):
            greet(barrier, [device])

        count = count + jnp.where(used, 1, 0)
    return count


def gather_kernel(
    points_hbm, noise, direction_hbm,
    got_points, got_dir, other_points, other_dir, image, other_image,
    far_first, code,
    points, direction, left, right, cols, near, column, rows, vis_rows, near_t, far_now,
    send_sem, recv_sem, local_sem,
):
    me = lax.axis_index("dev")
    p, comes_from, goes_to = visit_routes(me)
    barrier = pltpu.get_barrier_semaphore()
    count = greet_neighbours(barrier, me)
    load_points = pltpu.make_async_copy(points_hbm, points, local_sem.at[0])
    load_dir = pltpu.make_async_copy(direction_hbm, direction, local_sem.at[1])
    load_points.start()
    load_dir.start()

    def remote(src, dst, slot, part, to):
        return pltpu.make_async_remote_copy(
            src_ref=src,
            dst_ref=dst,
            send_sem=send_sem.at[slot, part],
            recv_sem=recv_sem.at[slot, part],
            device_id=(to,),
            device_id_type=MESH,
        )

    mate = [
        remote(points_hbm, other_points, SLOTS, 0, me + 1 - 2 * p),
        remote(direction_hbm, other_dir, SLOTS, 1, me + 1 - 2 * p),
    ]
    visits = [
        [
            remote(points_hbm, got_points.at[slot], slot, 0, goes_to[slot][0]),
            remote(direction_hbm, got_dir.at[slot], slot, 1, goes_to[slot][0]),
        ]
        for slot in range(SLOTS)
    ]

    def send(slot):
        @pl.when(goes_to[slot][1])
        def _():
            for copy in visits[slot]:
                copy.start()

    def receive(slot):
        @pl.when(comes_from[slot][1])
        def _():
            for copy in visits[slot]:
                copy.wait_recv()

        @pl.when(jnp.logical_not(comes_from[slot][1]))
        def _():
            got_points[slot] = other_points[...]
            got_dir[slot] = other_dir[...]

    load_points.wait()
    load_dir.wait()
    own = points[...]
    a, b = features(own, 0.0, True)
    left[...] = a.T.astype(BF)
    right[...] = b.astype(BF)
    set_rows(direction[...], direction[...], cols, rows, vis_rows)
    column[...] = jnp.broadcast_to(points[0:1, :], (128, N)).T
    image[...] = noise[...] * direction[...]
    extent = [extent_of(points[0:1, :])]
    near[...] = jnp.zeros_like(near)
    pl.semaphore_wait(barrier, count)
    for copy in mate:
        copy.start()
    send(0)
    send(3)
    for j in range(N // C):
        at_col, size = slice(j * C, (j + 1) * C), (j + 1) * C
        d = dot(left[:size, :], right[:, at_col])
        x = jnp.concatenate([column[:size, :]] * (C // 128), axis=1)
        x = x - points[0:1, at_col]
        high, low = halves(kern(d + x * x))
        near[:size, :] += dot(high, cols[at_col, :])
        image[:, :size] += fold(dot_t(rows[:, at_col], low))
        if j:
            mine = rows[:, : j * C]
            far = dot(mine, high[: j * C]) + dot(mine, low[: j * C])
            image[:, at_col] += fold(far)
    image[...] += fold(near[...].T)
    for copy in mate:
        copy.wait()
    receive(0)
    receive(3)
    send(2)
    send(1)

    other = other_points[...]
    extent.append(extent_of(other[0:1, :]))
    visits_at = {1: extent[1]}
    for slot in (0, 3):
        visits_at[slot] = extent_of(got_points[slot, 0:1, :])
    pf = p.astype(F)
    early = [(0, 0), (0, 1), (3, 0), (3, 1), (1, 0)]
    flags = []
    for slot, which in early:
        here = jnp.where(comes_from[slot][1], 1.0, 0.0)
        may = pf if slot == 1 else met(slot, which, pf) * here
        flags.append(apart(extent[which], visits_at[slot]) * may)
    picked = pick(flags)
    of_slot = {0: picked[0] + picked[1], 1: picked[4], 3: picked[2] + picked[3]}
    of_other = picked[1] + picked[3]
    visitor = choose(of_slot[1], other, got_points[0])
    visitor = choose(of_slot[3], got_points[3], visitor)
    visitor_dir = choose(of_slot[1], other_dir[...], got_dir[0])
    visitor_dir = choose(of_slot[3], got_dir[3], visitor_dir)
    host = choose(of_other, other, own)
    host_dir = choose(of_other, other_dir[...], direction[...])
    result = one_tile(
        host, host_dir, visitor, visitor_dir,
        left, right, cols, rows, vis_rows, near, near_t, far_now,
    )
    of_own = picked[0] + picked[2] + picked[4]
    image[...] += choose(of_own, result, jnp.zeros_like(result))
    other_image[...] = choose(of_other, result, jnp.zeros_like(result))
    for slot in range(SLOTS):
        if slot in of_slot:
            far_first[slot] = choose(of_slot[slot], far_now[...], jnp.zeros_like(result))
        else:
            far_first[slot] = jnp.zeros_like(result)
    receive(2)
    receive(1)
    for slot in (1, 2):
        visits_at[slot] = extent_of(got_points[slot, 0:1, :])

    flags = []
    for slot, which in LATE:
        if (slot, which) == (1, 0):
            may = pf * (1.0 - picked[4])
        else:
            may = met(slot, which, pf) * jnp.where(comes_from[slot][1], 1.0, 0.0)
        flags.append(apart(extent[which], visits_at[slot]) * may)
    late = pick(flags)
    code[...] = jnp.zeros_like(code)
    for (slot, which), here in zip(early, picked, strict=True):
        at = 2 * slot + which
        code[at : at + 1, :] += jnp.broadcast_to(here, (1, 128))
    for (slot, which), here in zip(LATE, late, strict=True):
        at = 2 * slot + which
        code[at : at + 1, :] += jnp.broadcast_to(2.0 * here, (1, 128))
    for slot in range(SLOTS):

        @pl.when(goes_to[slot][1])
        def _(slot=slot):
            for copy in visits[slot]:
                copy.wait_send()


def pair_kernel(
    place, pattern, code, points, direction, got_points, got_dir, other_points, other_dir,
    start, other_start, far_first, image, other_image, far_out,
    right, cols, near, near_t, left, column, vis_points, rows, vis_rows, far_now, total,
    extent,
):
    me = place[0]
    p = lax.rem(me, 2)
    firsts = [points[0:1, :], other_points[0:1, :]]
    firsts += [got_points[slot, 0:1, :] for slot in range(SLOTS)]
    for at, first in enumerate(firsts):
        extent[at, 0] = jnp.min(first)
        extent[at, 1] = jnp.max(first)
    far_out[...] = far_first[...]
    total[0] = start[...]
    total[1] = other_start[...]

    def one_pair(k, carry):
        slot, which = k // 2, lax.rem(k, 2)
        met_own = (slot == 0) | ((slot < 3) & (p == 1)) | ((slot == 3) & (p == 0))
        met_other = (slot != 1) | (p == 0)
        own_flag = (slot != 0) | (pattern[0, 1] > 0)
        ahead = me + jnp.where(slot == 0, 2, 4)
        behind = me - 2 * p - jnp.where(slot == 2, 3, 5)
        inside = ((slot == 1) & (p == 1)) | ((slot < 2) & (ahead < DEVS))
        inside = inside | ((slot >= 2) & (behind >= 0))
        allowed = ((which == 0) & met_own & own_flag) | ((which == 1) & met_other)
        allowed = allowed & inside

        theirs = slot + 2
        low, high = extent[theirs, 0], extent[theirs, 1]
        least, most = extent[which, 0], extent[which, 1]
        centre_s = 0.5 * least + 0.5 * most
        touch = (low - most < 1.0) & (least - high < 1.0)
        reach = jnp.maximum(jnp.maximum(high - centre_s, centre_s - low), most - least)
        narrow = reach <= NARROW
        left_over = code[k, 0] < 0.5

        @pl.when(allowed & touch & left_over)
        def _():
            own = which == 0
            visitor, visitor_dir = got_points[slot], got_dir[slot]
            host = jnp.where(own, points[...], other_points[...])
            host_dir = jnp.where(own, direction[...], other_dir[...])

            @pl.when(narrow)
            def _():
                total[which] += one_tile(
                    host, host_dir, visitor, visitor_dir,
                    left, right, cols, rows, vis_rows, near, near_t, far_now,
                )
                far_out[slot] += far_now[...]

            @pl.when(jnp.logical_not(narrow))
            def _():
                mine = host[0:1, :]
                a, _ = features(host, 0.0, True)
                left[...] = a.T.astype(BF)
                column[...] = jnp.broadcast_to(mine, (8, N)).T
                _, b = features(visitor, 0.0, True)
                right[...] = b.astype(BF)
                vis_points[...] = visitor
                set_rows(host_dir, visitor_dir, cols, rows, vis_rows)
                near[...] = jnp.zeros_like(near)

                def one_column(j, c):
                    at_col = pl.ds(pl.multiple_of(j * C, C), C)

                    def one_row(i, acc):
                        at_row = pl.ds(pl.multiple_of(i * C, C), C)
                        d = dot(left[at_row, :], right[:, at_col])
                        x = column[at_row, 0:1] - vis_points[0:1, at_col]
                        high, low = halves(kern(d + x * x))
                        w = cols[at_col, :]
                        near[at_row, :] += dot(high, w) + dot(low, w)
                        mine = rows[:, at_row]
                        return acc + dot(mine, high) + dot(mine, low)

                    far = lax.fori_loop(
                        0, N // C, one_row, jnp.zeros((2 * RHS, C), F)
                    )
                    far_out[slot, :, at_col] += fold(far)
                    return c

                lax.fori_loop(0, N // C, one_column, 0)
                total[which] += fold(near[...].T)

        return carry

    lax.fori_loop(0, 2 * SLOTS, one_pair, 0)

    image[...] = total[0]
    other_image[...] = total[1]


def finish_kernel(
    partial, other_partial, far, residual, direction, code, points, got_points, got_dir,
    other_points, other_dir, image, factors,
    got, sums, sum_got, other_image, far_last,
    left, right, cols, rows, vis_rows, near, near_t, far_now,
    send_sem, recv_sem, sum_send, sum_recv,
):
    me = lax.axis_index("dev")
    p, comes_from, goes_to = visit_routes(me)

    def partner(axis, k):
        stride, size = AXES[axis]
        at = lax.rem(me // stride, size)
        return me + (lax.rem(at + k, size) - at) * stride

    barrier = pltpu.get_barrier_semaphore()
    count = greet_neighbours(barrier, me)
    for axis, (_, size) in enumerate(AXES):
        greet(barrier, [partner(axis, k) for k in range(1, size)])
        count = count + (size - 1)
    pl.semaphore_wait(barrier, count)

    def remote(src, slot, to, part=0, columns=slice(0, N)):
        return pltpu.make_async_remote_copy(
            src_ref=src.at[:, columns],
            dst_ref=got.at[slot, :, columns],
            send_sem=send_sem.at[slot, part],
            recv_sem=recv_sem.at[slot, part],
            device_id=(to,),
            device_id_type=MESH,
        )

    most = slice(0, CUT * C)
    returns = [
        [
            remote(far_last.at[slot - 1], slot, to, 0, most),
            remote(far_last.at[slot - 1], slot, to, 1, slice(CUT * C, N)),
        ]
        if slot in (1, 2)
        else [remote(far.at[slot], slot, to)]
        for slot, (to, _) in enumerate(comes_from)
    ]
    mate = remote(other_image, SLOTS, me + 1 - 2 * p)

    def send(slot, part):
        pl.when(comes_from[slot][1])(returns[slot][part].start)

    send(0, 0)
    send(3, 0)
    r, d = residual[...], direction[...]
    rr = jnp.sum(r * r, axis=1, keepdims=True)

    late = [
        jnp.where(code[2 * slot + which : 2 * slot + which + 1, 0:1] > 1.5, 1.0, 0.0)
        for slot, which in LATE
    ]
    of_slot = {1: late[0] + late[1], 2: late[2] + late[3]}
    of_own, of_other = late[0] + late[2], late[1] + late[3]

    def send_done(steps):
        if steps not in (CUT, N // C):
            return
        part, columns = (0, most) if steps == CUT else (1, slice(CUT * C, N))
        now = far_now[:, columns]
        for slot in (2, 1):
            last = far[slot, :, columns] + choose(of_slot[slot], now, jnp.zeros_like(now))
            far_last[slot - 1, :, columns] = last
            send(slot, part)

    result = one_tile(
        choose(of_other, other_points[...], points[...]),
        choose(of_other, other_dir[...], d),
        choose(of_slot[1], got_points[1], got_points[2]),
        choose(of_slot[1], got_dir[1], got_dir[2]),
        left, right, cols, rows, vis_rows, near, near_t, far_now, send_done,
    )
    nothing = jnp.zeros_like(result)
    other = other_partial[...] + choose(of_other, result, nothing)
    other_image[...] = other + jnp.where(p == 1, far_last[0], 0.0)
    mate.start()
    image[...] = partial[...] + choose(of_own, result, nothing)
    mate.wait()
    image[...] += got[SLOTS]
    for slot in (0, 3, 1, 2):

        @pl.when(goes_to[slot][1])
        def _(slot=slot):
            for copy in returns[slot]:
                copy.wait_recv()
            image[...] += got[slot]

    total = image[...]
    curv = jnp.sum(d * total, axis=1, keepdims=True)
    cross = jnp.sum(r * total, axis=1, keepdims=True)
    square = jnp.sum(total * total, axis=1, keepdims=True)
    lane = lax.broadcasted_iota(jnp.int32, (RHS, 128), 1)
    sums[0] = jnp.where(
        lane == 0, rr, jnp.where(lane == 1, curv, jnp.where(lane == 2, cross, square))
    )
    at = 0
    leaving = []
    for axis, (_, size) in enumerate(AXES):
        started = []
        for k in range(1, size):
            copy = pltpu.make_async_remote_copy(
                src_ref=sums.at[axis],
                dst_ref=sum_got.at[at],
                send_sem=sum_send.at[at],
                recv_sem=sum_recv.at[at],
                device_id=(partner(axis, k),),
                device_id_type=MESH,
            )
            copy.start()
            started.append((copy, at))
            at += 1
        acc = sums[axis]
        for copy, place in started:
            copy.wait_recv()
            acc = acc + sum_got[place]
        sums[axis + 1] = acc
        leaving += [copy for copy, _ in started]
    result = sums[len(AXES)]
    rr, curv = result[:, 0:1], result[:, 1:2]
    cross, square = result[:, 2:3], result[:, 3:4]
    alpha = rr / curv
    fresh = jnp.maximum(rr - alpha * (2.0 * cross - alpha * square), 0.0)
    beta = fresh / (rr + 1e-05)
    factors[0] = jnp.broadcast_to(alpha, (RHS, 128))
    factors[1] = jnp.broadcast_to(beta, (RHS, 128))
    for copy in leaving:
        copy.wait_send()
    for slot in range(SLOTS):

        @pl.when(comes_from[slot][1])
        def _(slot=slot):
            for copy in returns[slot]:
                copy.wait_send()


def update_kernel(
    factors, image, solution, residual, direction, new_solution, new_residual, new_dir
):
    alpha, beta = factors[0, :, 0:1], factors[1, :, 0:1]
    d = direction[...]
    new_solution[...] = solution[...] + alpha * d
    r = residual[...] - alpha * image[...]
    new_residual[...] = r
    new_dir[...] = r + beta * d


def local(points, noise, pattern, solution, residual, direction):
    vmem = pl.BlockSpec(memory_space=pltpu.VMEM)
    hbm = pl.BlockSpec(memory_space=pl.ANY)
    smem = pl.BlockSpec(memory_space=pltpu.SMEM)
    shape = jax.ShapeDtypeStruct
    dma = pltpu.SemaphoreType.DMA
    (
        got_points, got_dir, other_points, other_dir, start, other_start, far_first, code,
    ) = pl.pallas_call(
        gather_kernel,
        out_shape=(
            shape((SLOTS, DIMS, N), F),
            shape((SLOTS, RHS, N), F),
            shape((DIMS, N), F),
            shape((RHS, N), F),
            shape((RHS, N), F),
            shape((RHS, N), F),
            shape((SLOTS, RHS, N), F),
            shape((2 * SLOTS, 128), F),
        ),
        in_specs=[hbm, vmem, hbm],
        out_specs=(vmem,) * 8,
        scratch_shapes=[
            pltpu.VMEM((DIMS, N), F),
            pltpu.VMEM((RHS, N), F),
            pltpu.VMEM((N, DEPTH), BF),
            pltpu.VMEM((DEPTH, N), BF),
            pltpu.VMEM((N, 2 * RHS), BF),
            pltpu.VMEM((N, 2 * RHS), F),
            pltpu.VMEM((N, 128), F),
            pltpu.VMEM((2 * RHS, N), BF),
            pltpu.VMEM((2 * RHS, N), BF),
            pltpu.VMEM((2 * RHS, N), F),
            pltpu.VMEM((RHS, N), F),
            dma((SLOTS + 1, 2)),
            dma((SLOTS + 1, 2)),
            dma((2,)),
        ],
        compiler_params=pltpu.CompilerParams(
            collective_id=0, has_side_effects=True, vmem_limit_bytes=VMEM_LIMIT
        ),
        name="gather_diagonal",
    )(points, noise.reshape(1, N), direction)
    place = lax.axis_index("dev").reshape(1).astype(jnp.int32)
    partial, other_image, far = pl.pallas_call(
        pair_kernel,
        out_shape=(
            shape((RHS, N), F),
            shape((RHS, N), F),
            shape((SLOTS, RHS, N), F),
        ),
        in_specs=[smem] * 3 + [vmem] * 9,
        out_specs=(vmem, vmem, vmem),
        scratch_shapes=[
            pltpu.VMEM((DEPTH, N), BF),
            pltpu.VMEM((N, 2 * RHS), BF),
            pltpu.VMEM((N, 2 * RHS), F),
            pltpu.VMEM((2 * RHS, N), F),
            pltpu.VMEM((N, DEPTH), BF),
            pltpu.VMEM((N, 8), F),
            pltpu.VMEM((DIMS, N), F),
            pltpu.VMEM((2 * RHS, N), BF),
            pltpu.VMEM((2 * RHS, N), BF),
            pltpu.VMEM((RHS, N), F),
            pltpu.VMEM((2, RHS, N), F),
            pltpu.SMEM((SLOTS + 2, 2), F),
        ],
        compiler_params=pltpu.CompilerParams(vmem_limit_bytes=VMEM_LIMIT),
        name="pairs",
    )(
        place, pattern, code, points, direction, got_points, got_dir, other_points,
        other_dir, start, other_start, far_first,
    )
    exchanges = sum(size - 1 for _, size in AXES)
    image, factors = pl.pallas_call(
        finish_kernel,
        out_shape=(shape((RHS, N), F), shape((2, RHS, 128), F)),
        in_specs=[vmem] * 11,
        out_specs=(vmem, vmem),
        scratch_shapes=[
            pltpu.VMEM((SLOTS + 1, RHS, N), F),
            pltpu.VMEM((len(AXES) + 1, RHS, 128), F),
            pltpu.VMEM((exchanges, RHS, 128), F),
            pltpu.VMEM((RHS, N), F),
            pltpu.VMEM((2, RHS, N), F),
            pltpu.VMEM((N, DEPTH), BF),
            pltpu.VMEM((DEPTH, N), BF),
            pltpu.VMEM((N, 2 * RHS), BF),
            pltpu.VMEM((2 * RHS, N), BF),
            pltpu.VMEM((2 * RHS, N), BF),
            pltpu.VMEM((N, 2 * RHS), F),
            pltpu.VMEM((2 * RHS, N), F),
            pltpu.VMEM((RHS, N), F),
            dma((SLOTS + 1, 2)),
            dma((SLOTS + 1, 2)),
            dma((exchanges,)),
            dma((exchanges,)),
        ],
        compiler_params=pltpu.CompilerParams(
            collective_id=1, has_side_effects=True, vmem_limit_bytes=VMEM_LIMIT
        ),
        name="finish",
    )(
        partial, other_image, far, residual, direction, code, points, got_points,
        got_dir, other_points, other_dir,
    )
    return pl.pallas_call(
        update_kernel,
        out_shape=(shape((RHS, N), F),) * 3,
        in_specs=[vmem] * 5,
        out_specs=(vmem,) * 3,
        name="update",
    )(factors, image, solution, residual, direction)


def solution(mesh):
    return jax.shard_map(
        local,
        mesh=mesh,
        in_specs=(
            P(None, "dev"),
            P("dev"),
            P("dev", None),
            P(None, "dev"),
            P(None, "dev"),
            P(None, "dev"),
        ),
        out_specs=(P(None, "dev"), P(None, "dev"), P(None, "dev")),
        check_vma=False,
    )
```

```python
import jax
import jax.numpy as jnp
from jax import lax
from jax.experimental import pallas as pl
from jax.experimental.pallas import tpu as pltpu
from jax.sharding import PartitionSpec as P

F = jnp.float32
BF = jnp.bfloat16
MESH = pl.DeviceIdType.MESH
DIMS = 8
RHS = 16
N = 2048
DEVS = 256
DEPTH = 64
C = 256
VMEM_LIMIT = 22 * 2**20
AXES = ((1, 2), (2, 4), (8, 4), (32, 8))

SLOTS = 4
CUT = 6
LATE = ((1, 0), (1, 1), (2, 0), (2, 1))
NARROW = 1.5


def split2(x):
    high = x.astype(BF)
    low = (x - high.astype(F)).astype(BF)
    return high.astype(F), low.astype(F)


def split3(x):
    high = x.astype(BF).astype(F)
    rest = x - high
    mid = rest.astype(BF).astype(F)
    low = (rest - mid).astype(BF).astype(F)
    return high, mid, low


def features(points, centre, skip_first):
    row = lax.broadcasted_iota(jnp.int32, points.shape, 0)
    x = jnp.where(row == 0, 0.0 if skip_first else points - centre, points - 0.5)
    norm = jnp.sum(x * x, axis=0, keepdims=True)
    a, b, c = split3(x)
    na, nb, nc = split3(norm)
    ones = jnp.where(row < 3, 1.0, 0.0)
    ones2 = jnp.where((row >= 3) & (row < 6), 1.0, 0.0)
    here = jnp.where(
        row == 0, na, jnp.where(row == 1, nb, jnp.where(row == 2, nc, ones2))
    )
    there = jnp.where(
        row == 3, na, jnp.where(row == 4, nb, jnp.where(row == 5, nc, ones))
    )
    zero = jnp.zeros_like(x)
    left = jnp.concatenate([a, a, b, b, a, c, here, zero], axis=0)
    right = jnp.concatenate(
        [-2.0 * a, -2.0 * b, -2.0 * a, -2.0 * b, -2.0 * c, -2.0 * a, there, zero],
        axis=0,
    )
    return left, right


def middle(first):
    least = jnp.min(first, axis=1, keepdims=True)
    most = jnp.max(first, axis=1, keepdims=True)
    return 0.5 * least + 0.5 * most


def halves_of_rows(direction):
    return jnp.concatenate(split2(direction * 7.0), axis=0)


def kern(dist_sq):
    u = jnp.minimum(jnp.maximum(dist_sq, 1e-30), 1.0)
    s = u * lax.rsqrt(u)
    t = 1.0 - s
    t2 = t * t
    return ((t2 * t2) * t2) * (t * (8.0 / 7.0 - t))


def halves(v):
    high = v.astype(BF)
    low = (v - high.astype(F)).astype(BF)
    return high, low


def fold(both):
    return both[:RHS] + both[RHS:]


def dot(a, b):
    return jnp.dot(a, b, preferred_element_type=F)


def dot_t(a, b):
    return lax.dot_general(a, b, (((1,), (1,)), ((), ())), preferred_element_type=F)


def extent_of(first):
    return jnp.min(first, axis=1, keepdims=True), jnp.max(first, axis=1, keepdims=True)


def apart(host, visitor):
    (least, most), (low, high) = host, visitor
    centre = 0.5 * least + 0.5 * most
    reach = jnp.maximum(jnp.maximum(high - centre, centre - low), most - least)
    touch = (low - most < 1.0) & (least - high < 1.0)
    return jnp.where(touch & (reach <= NARROW), 1.0, 0.0)


def choose(flag, value, other):
    return jnp.where(jnp.broadcast_to(flag, value.shape) > 0.0, value, other)


def met(slot, which, p):
    if which == 0:
        return (1.0, p, p, 1.0 - p)[slot]
    return (1.0, 1.0 - p, 1.0, 1.0)[slot]


def pick(flags):
    taken, picked = 0.0, []
    for flag in flags:
        here = flag * (1.0 - taken)
        taken = taken + here
        picked.append(here)
    return picked


def set_rows(host_dir, visitor_dir, cols, rows, vis_rows):
    rows[...] = halves_of_rows(host_dir).astype(BF)
    both = halves_of_rows(visitor_dir)
    vis_rows[...] = both.astype(BF)
    cols[...] = both.T.astype(BF)


def one_tile(host, host_dir, visitor, visitor_dir, left, right, cols, rows, vis_rows, near, near_t, far, after=None):
    centre = middle(host[0:1, :])
    a, _ = features(host, centre, False)
    left[...] = a.T.astype(BF)
    _, b = features(visitor, centre, False)
    right[...] = b.astype(BF)
    set_rows(host_dir, visitor_dir, cols, rows, vis_rows)
    for j in range(N // C):
        at_col = slice(j * C, (j + 1) * C)
        high, low = halves(kern(dot(left[...], right[:, at_col])))
        one = dot(high, cols[at_col, :])
        two = dot_t(vis_rows[:, at_col], low)
        near[...] = one if j == 0 else near[...] + one
        near_t[...] = two if j == 0 else near_t[...] + two
        far[:, at_col] = fold(dot(rows[...], high) + dot(rows[...], low))
        if after:
            after(j + 1)
    return fold(near[...].T + near_t[...])


def visit_routes(me):
    p = lax.rem(me, 2)

    def route(slot, by):
        there = me + by
        used = (there >= 0) & (there < DEVS)
        if slot == 1:
            used = used & (p == 0)
        return lax.rem(there + DEVS, DEVS), used

    comes_from = [route(i, by) for i, by in enumerate((2, 4, -3 - 2 * p, -5 - 2 * p))]
    goes_to = [route(i, by) for i, by in enumerate((-2, -4, 5 - 2 * p, 7 - 2 * p))]
    return p, comes_from, goes_to


def greet(barrier, targets):
    for target in targets:
        pl.semaphore_signal(barrier, inc=1, device_id=(target,), device_id_type=MESH)


def greet_neighbours(barrier, me):
    p, comes_from, goes_to = visit_routes(me)
    greet(barrier, [me + 1 - 2 * p])
    count = 1
    for device, used in comes_from + goes_to:

        @pl.when(used)
        def _(device=device):
            greet(barrier, [device])

        count = count + jnp.where(used, 1, 0)
    return count


def gather_kernel(
    points_hbm, noise, direction_hbm,
    got_points, got_dir, other_points, other_dir, image, other_image,
    far_first, code,
    points, direction, left, right, cols, near, column, rows, vis_rows, near_t, far_now,
    send_sem, recv_sem, local_sem,
):
    me = lax.axis_index("dev")
    p, comes_from, goes_to = visit_routes(me)
    barrier = pltpu.get_barrier_semaphore()
    count = greet_neighbours(barrier, me)
    load_points = pltpu.make_async_copy(points_hbm, points, local_sem.at[0])
    load_dir = pltpu.make_async_copy(direction_hbm, direction, local_sem.at[1])
    load_points.start()
    load_dir.start()

    def remote(src, dst, slot, part, to):
        return pltpu.make_async_remote_copy(
            src_ref=src,
            dst_ref=dst,
            send_sem=send_sem.at[slot, part],
            recv_sem=recv_sem.at[slot, part],
            device_id=(to,),
            device_id_type=MESH,
        )

    mate = [
        remote(points_hbm, other_points, SLOTS, 0, me + 1 - 2 * p),
        remote(direction_hbm, other_dir, SLOTS, 1, me + 1 - 2 * p),
    ]
    visits = [
        [
            remote(points_hbm, got_points.at[slot], slot, 0, goes_to[slot][0]),
            remote(direction_hbm, got_dir.at[slot], slot, 1, goes_to[slot][0]),
        ]
        for slot in range(SLOTS)
    ]

    def send(slot):
        @pl.when(goes_to[slot][1])
        def _():
            for copy in visits[slot]:
                copy.start()

    def receive(slot):
        @pl.when(comes_from[slot][1])
        def _():
            for copy in visits[slot]:
                copy.wait_recv()

        @pl.when(jnp.logical_not(comes_from[slot][1]))
        def _():
            got_points[slot] = other_points[...]
            got_dir[slot] = other_dir[...]

    load_points.wait()
    load_dir.wait()
    own = points[...]
    a, b = features(own, 0.0, True)
    left[...] = a.T.astype(BF)
    right[...] = b.astype(BF)
    set_rows(direction[...], direction[...], cols, rows, vis_rows)
    column[...] = jnp.broadcast_to(points[0:1, :], (128, N)).T
    image[...] = noise[...] * direction[...]
    extent = [extent_of(points[0:1, :])]
    near[...] = jnp.zeros_like(near)
    pl.semaphore_wait(barrier, count)
    for copy in mate:
        copy.start()
    send(0)
    send(3)
    for j in range(N // C):
        at_col, size = slice(j * C, (j + 1) * C), (j + 1) * C
        d = dot(left[:size, :], right[:, at_col])
        x = jnp.concatenate([column[:size, :]] * (C // 128), axis=1)
        x = x - points[0:1, at_col]
        high, low = halves(kern(d + x * x))
        near[:size, :] += dot(high, cols[at_col, :])
        image[:, :size] += fold(dot_t(rows[:, at_col], low))
        if j:
            mine = rows[:, : j * C]
            far = dot(mine, high[: j * C]) + dot(mine, low[: j * C])
            image[:, at_col] += fold(far)
    image[...] += fold(near[...].T)
    for copy in mate:
        copy.wait()
    receive(0)
    receive(3)
    send(2)
    send(1)

    other = other_points[...]
    extent.append(extent_of(other[0:1, :]))
    visits_at = {1: extent[1]}
    for slot in (0, 3):
        visits_at[slot] = extent_of(got_points[slot, 0:1, :])
    pf = p.astype(F)
    early = [(0, 0), (0, 1), (3, 0), (3, 1), (1, 0)]
    flags = []
    for slot, which in early:
        here = jnp.where(comes_from[slot][1], 1.0, 0.0)
        may = pf if slot == 1 else met(slot, which, pf) * here
        flags.append(apart(extent[which], visits_at[slot]) * may)
    picked = pick(flags)
    of_slot = {0: picked[0] + picked[1], 1: picked[4], 3: picked[2] + picked[3]}
    of_other = picked[1] + picked[3]
    visitor = choose(of_slot[1], other, got_points[0])
    visitor = choose(of_slot[3], got_points[3], visitor)
    visitor_dir = choose(of_slot[1], other_dir[...], got_dir[0])
    visitor_dir = choose(of_slot[3], got_dir[3], visitor_dir)
    host = choose(of_other, other, own)
    host_dir = choose(of_other, other_dir[...], direction[...])
    result = one_tile(
        host, host_dir, visitor, visitor_dir,
        left, right, cols, rows, vis_rows, near, near_t, far_now,
    )
    of_own = picked[0] + picked[2] + picked[4]
    image[...] += choose(of_own, result, jnp.zeros_like(result))
    other_image[...] = choose(of_other, result, jnp.zeros_like(result))
    for slot in range(SLOTS):
        if slot in of_slot:
            far_first[slot] = choose(of_slot[slot], far_now[...], jnp.zeros_like(result))
        else:
            far_first[slot] = jnp.zeros_like(result)
    receive(2)
    receive(1)
    for slot in (1, 2):
        visits_at[slot] = extent_of(got_points[slot, 0:1, :])

    flags = []
    for slot, which in LATE:
        if (slot, which) == (1, 0):
            may = pf * (1.0 - picked[4])
        else:
            may = met(slot, which, pf) * jnp.where(comes_from[slot][1], 1.0, 0.0)
        flags.append(apart(extent[which], visits_at[slot]) * may)
    late = pick(flags)
    code[...] = jnp.zeros_like(code)
    for (slot, which), here in zip(early, picked, strict=True):
        at = 2 * slot + which
        code[at : at + 1, :] += jnp.broadcast_to(here, (1, 128))
    for (slot, which), here in zip(LATE, late, strict=True):
        at = 2 * slot + which
        code[at : at + 1, :] += jnp.broadcast_to(2.0 * here, (1, 128))
    for slot in range(SLOTS):

        @pl.when(goes_to[slot][1])
        def _(slot=slot):
            for copy in visits[slot]:
                copy.wait_send()


def pair_kernel(
    place, pattern, code, points, direction, got_points, got_dir, other_points, other_dir,
    start, other_start, far_first, image, other_image, far_out,
    right, cols, near, near_t, left, column, vis_points, rows, vis_rows, far_now, total,
    extent,
):
    me = place[0]
    p = lax.rem(me, 2)
    firsts = [points[0:1, :], other_points[0:1, :]]
    firsts += [got_points[slot, 0:1, :] for slot in range(SLOTS)]
    for at, first in enumerate(firsts):
        extent[at, 0] = jnp.min(first)
        extent[at, 1] = jnp.max(first)
    far_out[...] = far_first[...]
    total[0] = start[...]
    total[1] = other_start[...]

    def one_pair(k, carry):
        slot, which = k // 2, lax.rem(k, 2)
        met_own = (slot == 0) | ((slot < 3) & (p == 1)) | ((slot == 3) & (p == 0))
        met_other = (slot != 1) | (p == 0)
        own_flag = (slot != 0) | (pattern[0, 1] > 0)
        ahead = me + jnp.where(slot == 0, 2, 4)
        behind = me - 2 * p - jnp.where(slot == 2, 3, 5)
        inside = ((slot == 1) & (p == 1)) | ((slot < 2) & (ahead < DEVS))
        inside = inside | ((slot >= 2) & (behind >= 0))
        allowed = ((which == 0) & met_own & own_flag) | ((which == 1) & met_other)
        allowed = allowed & inside

        theirs = slot + 2
        low, high = extent[theirs, 0], extent[theirs, 1]
        least, most = extent[which, 0], extent[which, 1]
        centre_s = 0.5 * least + 0.5 * most
        touch = (low - most < 1.0) & (least - high < 1.0)
        reach = jnp.maximum(jnp.maximum(high - centre_s, centre_s - low), most - least)
        narrow = reach <= NARROW
        left_over = code[k, 0] < 0.5

        @pl.when(allowed & touch & left_over)
        def _():
            own = which == 0
            visitor, visitor_dir = got_points[slot], got_dir[slot]
            host = jnp.where(own, points[...], other_points[...])
            host_dir = jnp.where(own, direction[...], other_dir[...])

            @pl.when(narrow)
            def _():
                total[which] += one_tile(
                    host, host_dir, visitor, visitor_dir,
                    left, right, cols, rows, vis_rows, near, near_t, far_now,
                )
                far_out[slot] += far_now[...]

            @pl.when(jnp.logical_not(narrow))
            def _():
                mine = host[0:1, :]
                a, _ = features(host, 0.0, True)
                left[...] = a.T.astype(BF)
                column[...] = jnp.broadcast_to(mine, (8, N)).T
                _, b = features(visitor, 0.0, True)
                right[...] = b.astype(BF)
                vis_points[...] = visitor
                set_rows(host_dir, visitor_dir, cols, rows, vis_rows)
                near[...] = jnp.zeros_like(near)

                def one_column(j, c):
                    at_col = pl.ds(pl.multiple_of(j * C, C), C)

                    def one_row(i, acc):
                        at_row = pl.ds(pl.multiple_of(i * C, C), C)
                        d = dot(left[at_row, :], right[:, at_col])
                        x = column[at_row, 0:1] - vis_points[0:1, at_col]
                        high, low = halves(kern(d + x * x))
                        w = cols[at_col, :]
                        near[at_row, :] += dot(high, w) + dot(low, w)
                        mine = rows[:, at_row]
                        return acc + dot(mine, high) + dot(mine, low)

                    far = lax.fori_loop(
                        0, N // C, one_row, jnp.zeros((2 * RHS, C), F)
                    )
                    far_out[slot, :, at_col] += fold(far)
                    return c

                lax.fori_loop(0, N // C, one_column, 0)
                total[which] += fold(near[...].T)

        return carry

    lax.fori_loop(0, 2 * SLOTS, one_pair, 0)

    image[...] = total[0]
    other_image[...] = total[1]


def finish_kernel(
    partial, other_partial, far, residual, direction, code, points, got_points, got_dir,
    other_points, other_dir, image, factors,
    got, sums, sum_got, other_image, far_last,
    left, right, cols, rows, vis_rows, near, near_t, far_now,
    send_sem, recv_sem, sum_send, sum_recv,
):
    me = lax.axis_index("dev")
    p, comes_from, goes_to = visit_routes(me)

    def partner(axis, k):
        stride, size = AXES[axis]
        at = lax.rem(me // stride, size)
        return me + (lax.rem(at + k, size) - at) * stride

    barrier = pltpu.get_barrier_semaphore()
    count = greet_neighbours(barrier, me)
    for axis, (_, size) in enumerate(AXES):
        greet(barrier, [partner(axis, k) for k in range(1, size)])
        count = count + (size - 1)
    pl.semaphore_wait(barrier, count)

    def remote(src, slot, to, part=0, columns=slice(0, N)):
        return pltpu.make_async_remote_copy(
            src_ref=src.at[:, columns],
            dst_ref=got.at[slot, :, columns],
            send_sem=send_sem.at[slot, part],
            recv_sem=recv_sem.at[slot, part],
            device_id=(to,),
            device_id_type=MESH,
        )

    most = slice(0, CUT * C)
    returns = [
        [
            remote(far_last.at[slot - 1], slot, to, 0, most),
            remote(far_last.at[slot - 1], slot, to, 1, slice(CUT * C, N)),
        ]
        if slot in (1, 2)
        else [remote(far.at[slot], slot, to)]
        for slot, (to, _) in enumerate(comes_from)
    ]
    mate = remote(other_image, SLOTS, me + 1 - 2 * p)

    def send(slot, part):
        pl.when(comes_from[slot][1])(returns[slot][part].start)

    send(0, 0)
    send(3, 0)
    r, d = residual[...], direction[...]
    rr = jnp.sum(r * r, axis=1, keepdims=True)

    late = [
        jnp.where(code[2 * slot + which : 2 * slot + which + 1, 0:1] > 1.5, 1.0, 0.0)
        for slot, which in LATE
    ]
    of_slot = {1: late[0] + late[1], 2: late[2] + late[3]}
    of_own, of_other = late[0] + late[2], late[1] + late[3]

    def send_done(steps):
        if steps not in (CUT, N // C):
            return
        part, columns = (0, most) if steps == CUT else (1, slice(CUT * C, N))
        now = far_now[:, columns]
        for slot in (2, 1):
            last = far[slot, :, columns] + choose(of_slot[slot], now, jnp.zeros_like(now))
            far_last[slot - 1, :, columns] = last
            send(slot, part)

    result = one_tile(
        choose(of_other, other_points[...], points[...]),
        choose(of_other, other_dir[...], d),
        choose(of_slot[1], got_points[1], got_points[2]),
        choose(of_slot[1], got_dir[1], got_dir[2]),
        left, right, cols, rows, vis_rows, near, near_t, far_now, send_done,
    )
    nothing = jnp.zeros_like(result)
    other = other_partial[...] + choose(of_other, result, nothing)
    other_image[...] = other + jnp.where(p == 1, far_last[0], 0.0)
    mate.start()
    image[...] = partial[...] + choose(of_own, result, nothing)
    mate.wait()
    image[...] += got[SLOTS]
    for slot in (0, 3, 1, 2):

        @pl.when(goes_to[slot][1])
        def _(slot=slot):
            for copy in returns[slot]:
                copy.wait_recv()
            image[...] += got[slot]

    total = image[...]
    curv = jnp.sum(d * total, axis=1, keepdims=True)
    cross = jnp.sum(r * total, axis=1, keepdims=True)
    square = jnp.sum(total * total, axis=1, keepdims=True)
    lane = lax.broadcasted_iota(jnp.int32, (RHS, 128), 1)
    sums[0] = jnp.where(
        lane == 0, rr, jnp.where(lane == 1, curv, jnp.where(lane == 2, cross, square))
    )
    at = 0
    leaving = []
    for axis, (_, size) in enumerate(AXES):
        started = []
        for k in range(1, size):
            copy = pltpu.make_async_remote_copy(
                src_ref=sums.at[axis],
                dst_ref=sum_got.at[at],
                send_sem=sum_send.at[at],
                recv_sem=sum_recv.at[at],
                device_id=(partner(axis, k),),
                device_id_type=MESH,
            )
            copy.start()
            started.append((copy, at))
            at += 1
        acc = sums[axis]
        for copy, place in started:
            copy.wait_recv()
            acc = acc + sum_got[place]
        sums[axis + 1] = acc
        leaving += [copy for copy, _ in started]
    result = sums[len(AXES)]
    rr, curv = result[:, 0:1], result[:, 1:2]
    cross, square = result[:, 2:3], result[:, 3:4]
    alpha = rr / curv
    fresh = jnp.maximum(rr - alpha * (2.0 * cross - alpha * square), 0.0)
    beta = fresh / (rr + 1e-05)
    factors[0] = jnp.broadcast_to(alpha, (RHS, 128))
    factors[1] = jnp.broadcast_to(beta, (RHS, 128))
    for copy in leaving:
        copy.wait_send()
    for slot in range(SLOTS):

        @pl.when(comes_from[slot][1])
        def _(slot=slot):
            for copy in returns[slot]:
                copy.wait_send()


def update_kernel(
    factors, image, solution, residual, direction, new_solution, new_residual, new_dir
):
    alpha, beta = factors[0, :, 0:1], factors[1, :, 0:1]
    d = direction[...]
    new_solution[...] = solution[...] + alpha * d
    r = residual[...] - alpha * image[...]
    new_residual[...] = r
    new_dir[...] = r + beta * d


def local(points, noise, pattern, solution, residual, direction):
    vmem = pl.BlockSpec(memory_space=pltpu.VMEM)
    hbm = pl.BlockSpec(memory_space=pl.ANY)
    smem = pl.BlockSpec(memory_space=pltpu.SMEM)
    shape = jax.ShapeDtypeStruct
    dma = pltpu.SemaphoreType.DMA
    (
        got_points, got_dir, other_points, other_dir, start, other_start, far_first, code,
    ) = pl.pallas_call(
        gather_kernel,
        out_shape=(
            shape((SLOTS, DIMS, N), F),
            shape((SLOTS, RHS, N), F),
            shape((DIMS, N), F),
            shape((RHS, N), F),
            shape((RHS, N), F),
            shape((RHS, N), F),
            shape((SLOTS, RHS, N), F),
            shape((2 * SLOTS, 128), F),
        ),
        in_specs=[hbm, vmem, hbm],
        out_specs=(vmem,) * 8,
        scratch_shapes=[
            pltpu.VMEM((DIMS, N), F),
            pltpu.VMEM((RHS, N), F),
            pltpu.VMEM((N, DEPTH), BF),
            pltpu.VMEM((DEPTH, N), BF),
            pltpu.VMEM((N, 2 * RHS), BF),
            pltpu.VMEM((N, 2 * RHS), F),
            pltpu.VMEM((N, 128), F),
            pltpu.VMEM((2 * RHS, N), BF),
            pltpu.VMEM((2 * RHS, N), BF),
            pltpu.VMEM((2 * RHS, N), F),
            pltpu.VMEM((RHS, N), F),
            dma((SLOTS + 1, 2)),
            dma((SLOTS + 1, 2)),
            dma((2,)),
        ],
        compiler_params=pltpu.CompilerParams(
            collective_id=0, has_side_effects=True, vmem_limit_bytes=VMEM_LIMIT
        ),
        name="gather_diagonal",
    )(points, noise.reshape(1, N), direction)
    place = lax.axis_index("dev").reshape(1).astype(jnp.int32)
    partial, other_image, far = pl.pallas_call(
        pair_kernel,
        out_shape=(
            shape((RHS, N), F),
            shape((RHS, N), F),
            shape((SLOTS, RHS, N), F),
        ),
        in_specs=[smem] * 3 + [vmem] * 9,
        out_specs=(vmem, vmem, vmem),
        scratch_shapes=[
            pltpu.VMEM((DEPTH, N), BF),
            pltpu.VMEM((N, 2 * RHS), BF),
            pltpu.VMEM((N, 2 * RHS), F),
            pltpu.VMEM((2 * RHS, N), F),
            pltpu.VMEM((N, DEPTH), BF),
            pltpu.VMEM((N, 8), F),
            pltpu.VMEM((DIMS, N), F),
            pltpu.VMEM((2 * RHS, N), BF),
            pltpu.VMEM((2 * RHS, N), BF),
            pltpu.VMEM((RHS, N), F),
            pltpu.VMEM((2, RHS, N), F),
            pltpu.SMEM((SLOTS + 2, 2), F),
        ],
        compiler_params=pltpu.CompilerParams(vmem_limit_bytes=VMEM_LIMIT),
        name="pairs",
    )(
        place, pattern, code, points, direction, got_points, got_dir, other_points,
        other_dir, start, other_start, far_first,
    )
    exchanges = sum(size - 1 for _, size in AXES)
    image, factors = pl.pallas_call(
        finish_kernel,
        out_shape=(shape((RHS, N), F), shape((2, RHS, 128), F)),
        in_specs=[vmem] * 11,
        out_specs=(vmem, vmem),
        scratch_shapes=[
            pltpu.VMEM((SLOTS + 1, RHS, N), F),
            pltpu.VMEM((len(AXES) + 1, RHS, 128), F),
            pltpu.VMEM((exchanges, RHS, 128), F),
            pltpu.VMEM((RHS, N), F),
            pltpu.VMEM((2, RHS, N), F),
            pltpu.VMEM((N, DEPTH), BF),
            pltpu.VMEM((DEPTH, N), BF),
            pltpu.VMEM((N, 2 * RHS), BF),
            pltpu.VMEM((2 * RHS, N), BF),
            pltpu.VMEM((2 * RHS, N), BF),
            pltpu.VMEM((N, 2 * RHS), F),
            pltpu.VMEM((2 * RHS, N), F),
            pltpu.VMEM((RHS, N), F),
            dma((SLOTS + 1, 2)),
            dma((SLOTS + 1, 2)),
            dma((exchanges,)),
            dma((exchanges,)),
        ],
        compiler_params=pltpu.CompilerParams(
            collective_id=1, has_side_effects=True, vmem_limit_bytes=VMEM_LIMIT
        ),
        name="finish",
    )(
        partial, other_image, far, residual, direction, code, points, got_points,
        got_dir, other_points, other_dir,
    )
    return pl.pallas_call(
        update_kernel,
        out_shape=(shape((RHS, N), F),) * 3,
        in_specs=[vmem] * 5,
        out_specs=(vmem,) * 3,
        compiler_params=pltpu.CompilerParams(vmem_limit_bytes=56 * 2**20),
        name="update",
    )(factors, image, solution, residual, direction)


def solution(mesh):
    return jax.shard_map(
        local,
        mesh=mesh,
        in_specs=(
            P(None, "dev"),
            P("dev"),
            P("dev", None),
            P(None, "dev"),
            P(None, "dev"),
            P(None, "dev"),
        ),
        out_specs=(P(None, "dev"), P(None, "dev"), P(None, "dev")),
        check_vma=False,
    )
```
